32 devices in a mesh: dp: 4 (over y, x), expert: 8 (over z, core).
Axes of the slice: x: 2, y: 2, z: 4, core: 2. Of those that a mesh axis runs over, the one named last changes fastest.
Arguments:
- tokens: bfloat16 [4096, 2048], P(('dp', 'expert')), may hold values from -6 to 6
- routes: int32 [4096, 2], P(('dp', 'expert')), may hold values from 0 to 7, all different within a row; in each aligned block of 128 rows (0 to 127, 128 to 255, ...) at most 36 rows name the same one
- gates: int32 [4096, 2], P(('dp', 'expert')), may hold values from 1 to 1023
- cotangent: bfloat16 [4096, 2048], P(('dp', 'expert')), may hold values from -6 to 6
- w_gate: bfloat16 [2048, 8192], P(None, 'expert'), may hold values from -0.125 to 0.125
- w_up: bfloat16 [2048, 8192], P(None, 'expert'), may hold values from -0.125 to 0.125
- w_down: bfloat16 [8192, 2048], P('expert'), may hold values from -0.1875 to 0.1875
Outputs:
- mixed: bfloat16 [4096, 2048], P(('dp', 'expert'))
- input_grad: bfloat16 [4096, 2048], P(('dp', 'expert'))
- grad_gate: float32 [2048, 8192], P('dp', 'expert')
- grad_up: float32 [2048, 8192], P('dp', 'expert')
- grad_down: float32 [8192, 2048], P('expert', 'dp')
The draws below stay inside these ranges and needn't reach their ends.
Inputs may be any that keep to these rules, and one draw needn't show every extreme that they name: `routes`: the two experts of a token differ. In the rows of one device no expert is named by more than 36 pairs, a bound that some block reaches.
All inputs are finite; a program needn't handle non-finite values.
Results may differ from the reference program's by a relative error of at most 0.0064.
Values may be sent and summed in bfloat16 or wider, within the bound.
No kernel may reach another device: no remote copies, remote signals or barrier semaphores. Data moves between devices by JAX's collectives and lax.ppermute only.
A program may use at most 128 MiB of HBM per device.

```python
import math
import jax
import jax.numpy as jnp
import numpy as np
from jax import lax

D = 2048
FF = 1024
EXPERTS = 8
TOK_DEV = 128
CAP = 36
H = 1024
TOKENS = 4096
N_EXPERT = 8


def with_ends(array, key, least, high):
    longest = array.shape.index(max(array.shape))
    spots = []
    for shift in (0, 1):
        where = [jax.random.randint(jax.random.fold_in(key, axis), (), 0, length) for axis, length in enumerate(array.shape)]
        where[longest] = (where[longest] + shift) % array.shape[longest]
        spots.append(tuple(where))
    return array.at[spots[0]].set(least).at[spots[1]].set(high)


def spiked(array, stream_key, source, target, parts, factor):
    owner, partner = [(jnp.arange(array.shape[axis_at]) // (array.shape[axis_at] // parts)).reshape([-1 if axis == axis_at else 1 for axis in range(array.ndim)]) for axis_at in (source, target)]
    chosen = jax.random.permutation(stream_key, parts)[partner]
    strong = (owner == chosen) | (owner == (partner + parts // 2) % parts)
    return jnp.where(strong, factor * array, array)


def block_scale(key, extent, cuts, low, largest):
    gain = 1.0
    for dim, parts in cuts:
        steps = jax.random.uniform(jax.random.fold_in(jax.random.fold_in(key, 6), dim), (parts,), jnp.float32, low / len(cuts), largest / len(cuts))
        gain = gain * jnp.repeat(jnp.exp(steps), extent[dim] // parts).reshape((-1,) + (1,) * (len(extent) - 1 - dim))
    return gain


def routed_block(key, own, number, rows, amount, top, reach, skew):
    order = jax.random.permutation(key, amount)
    crowded, ordinary = load_shares(amount, rows * top, reach, skew, True), load_shares(amount, rows * top, reach, skew, False)
    places = jnp.arange(amount)

    def named(lengths, rotation):
        used = int((lengths > 0).sum())
        fixed = max(1, used // 4)
        moved = fixed + (places - fixed + rotation * (used - fixed)) % max(1, amount - fixed)
        return jnp.zeros((amount,), jnp.int32).at[order[jnp.where(places < fixed, places, moved)]].set(jnp.asarray(lengths, jnp.int32))

    lengths = jnp.where(number % 4 == 0, named(crowded, number // 4), named(ordinary, number - number // 4 - 1))
    mixed = jax.random.permutation(jax.random.fold_in(own, 3), amount)
    source_of, sink = mixed[0:amount // 2 * 2:2], mixed[1:amount // 2 * 2:2]
    slack = jnp.minimum(lengths[source_of] - 1, reach - lengths[sink]) // 2
    slack = jnp.where((source_of == order[0]) | (sink == order[0]) | (lengths[sink] == 0), 0, jnp.maximum(slack, 0))
    moved = jax.random.randint(jax.random.fold_in(own, 4), (amount // 2,), 0, 1 << 20) % (slack + 1)
    lengths = lengths.at[source_of].add(-moved).at[sink].add(moved)
    members = jnp.searchsorted(jnp.cumsum(lengths), jnp.arange(rows * top), side="right").astype(jnp.int32)
    table = members.reshape(top, rows).T
    table = table[jax.random.permutation(jax.random.fold_in(own, 1), rows)]
    rotation = jax.random.randint(jax.random.fold_in(own, 2), (rows, 1), 0, top)
    return jnp.take_along_axis(table, (jnp.arange(top)[None, :] + rotation) % top, axis=1)


def load_shares(amount, total, most, skew, full):
    loads = [(1 << 20) // math.isqrt(grade ** skew) + 1 for grade in range(1, amount + 1)]
    largest = most if full else min(most, max(-(-total // amount), total * loads[0] // sum(loads)))
    least = 1 if total - largest >= amount - 1 else 0
    holding, spare = [largest] + [least] * (amount - 1), total - largest - least * (amount - 1)
    while spare > 0:
        movable = [i for i in range(1, amount) if holding[i] < largest] or [i for i in range(1, amount) if holding[i] < most]
        pool, left = sum([loads[i] for i in movable]), spare
        for i in movable:
            more = min(most - holding[i], max(1, left * loads[i] // pool), spare)
            holding[i] = holding[i] + more
            spare = spare - more
    return np.array(holding)


def normal_values(rng, dims, spread, reach, shards=(), kind=jnp.bfloat16):
    values = jax.random.normal(rng, dims, jnp.float32) * spread
    if len(shards) > 0:
        values = block_scale(rng, dims, shards, -0.22, 0.18) * values
    return jnp.clip(values, min=-reach, max=reach).astype(kind)


def gaussian_with(own_key, dims, scale, reach, shards, heavy, held_as=jnp.bfloat16):
    values = scale * jax.random.normal(own_key, dims, jnp.float32)
    if shards:
        values = values * block_scale(own_key, dims, shards, -0.22, 0.18)
    return jnp.clip(spiked(values, jax.random.fold_in(own_key, 3), *heavy), -reach, reach).astype(held_as)


def setup_inputs(seed: int = 0) -> dict:
    arg_keys = jax.random.split(jax.random.key(seed), 8)
    tokens = gaussian_with(arg_keys[0], (TOKENS, D), 1.0, 6.0, ((0, 32),), (0, 1, 32, 2.75))
    routes_keys = jax.random.split(jax.random.fold_in(arg_keys[1], 1), TOKENS // TOK_DEV)
    routes_turns = jax.random.permutation(jax.random.fold_in(arg_keys[1], 3), TOKENS // TOK_DEV)
    routes = jax.vmap(lambda own, number: routed_block(jax.random.fold_in(arg_keys[1], 2), own, number, TOK_DEV, EXPERTS, 2, CAP, 2))(routes_keys, routes_turns).reshape((TOKENS, 2))
    gates = with_ends(jax.random.randint(arg_keys[2], (TOKENS, 2), 1, 1024), jax.random.fold_in(arg_keys[2], 1), 1, 1023).astype(jnp.int32)
    cotangent = normal_values(arg_keys[3], (TOKENS, D), 1.0, 6.0, ((0, 32),))
    w_gate = normal_values(arg_keys[4], (D, EXPERTS * FF), D ** -0.5, 0.125, ((1, 8),))
    w_up = normal_values(arg_keys[5], (D, EXPERTS * FF), D ** -0.5, 0.125, ((1, 8),))
    w_down = normal_values(arg_keys[6], (EXPERTS * FF, D), FF ** -0.5, 0.1875, ((0, 8),))
    return {"tokens": tokens, "routes": routes, "gates": gates, "cotangent": cotangent, "w_gate": w_gate, "w_up": w_up, "w_down": w_down}


def local_table(pairs):
    count = pairs.shape[0]
    onehot = (pairs[:, None] == jnp.arange(EXPERTS, dtype=jnp.int32)[None, :]).astype(jnp.int32)
    before = jnp.cumsum(onehot, axis=0) - onehot
    position = jnp.sum(before * onehot, axis=1).astype(jnp.int32)
    table = jnp.full((EXPERTS * CAP,), count, jnp.int32)
    return table.at[pairs * CAP + position].set(jnp.arange(count, dtype=jnp.int32))


def reference(tokens, routes, gates, cotangent, w_gate, w_up, w_down):
    blocks = TOKENS // TOK_DEV
    per = 2 * TOK_DEV
    tiles = N_EXPERT // EXPERTS
    tables = jax.vmap(local_table)(routes.reshape(blocks, per).astype(jnp.int32))
    offsets = (jnp.arange(blocks, dtype=jnp.int32) * per)[:, None]
    global_ids = jnp.where(tables < per, tables + offsets, 2 * TOKENS).astype(jnp.int32).reshape(blocks, EXPERTS, CAP)
    factor = jnp.concatenate([gates.reshape(-1).astype(jnp.float32) / 1024.0, jnp.zeros((1,), jnp.float32)])
    padded_x = jnp.concatenate([tokens, jnp.zeros((1, D), jnp.bfloat16)])
    padded_dy = jnp.concatenate([cotangent, jnp.zeros((1, D), jnp.bfloat16)])
    mixed_acc = jnp.zeros((TOKENS + 1, D), jnp.float32)
    dx_acc = jnp.zeros((TOKENS + 1, D), jnp.float32)
    gate_list, up_list, down_list = [], [], []
    for expert in range(EXPERTS):
        ids = global_ids[:, expert, :].reshape(-1)
        rows_tok = (ids // 2).astype(jnp.int32)
        xrows = padded_x[rows_tok]
        scale = factor[ids]
        dz = (scale[:, None] * padded_dy[rows_tok].astype(jnp.float32)).astype(jnp.bfloat16)
        for part in range(tiles):
            col = (expert * tiles + part) * H
            wg = w_gate[:, col:col + H]
            wu = w_up[:, col:col + H]
            wd = w_down[col:col + H, :]
            a = jnp.dot(xrows, wg, preferred_element_type=jnp.float32)
            b = jnp.dot(xrows, wu, preferred_element_type=jnp.float32)
            sig = jax.nn.sigmoid(a)
            act = a * sig
            h = (act * b).astype(jnp.bfloat16)
            z = jnp.dot(h, wd, preferred_element_type=jnp.float32).astype(jnp.bfloat16)
            mixed_acc = mixed_acc.at[rows_tok].add(scale[:, None] * z.astype(jnp.float32))
            dh = lax.dot_general(dz, wd, (((1,), (1,)), ((), ())), preferred_element_type=jnp.float32)
            dsilu = sig * (1.0 + a * (1.0 - sig))
            d_gate = (dh * b * dsilu).astype(jnp.bfloat16)
            d_up = (dh * act).astype(jnp.bfloat16)
            dx = lax.dot_general(d_gate, wg, (((1,), (1,)), ((), ())), preferred_element_type=jnp.float32)
            dx = dx + lax.dot_general(d_up, wu, (((1,), (1,)), ((), ())), preferred_element_type=jnp.float32)
            dx_acc = dx_acc.at[rows_tok].add(dx.astype(jnp.bfloat16).astype(jnp.float32))
            gate_list.append(lax.dot_general(xrows, d_gate, (((0,), (0,)), ((), ())), preferred_element_type=jnp.float32))
            up_list.append(lax.dot_general(xrows, d_up, (((0,), (0,)), ((), ())), preferred_element_type=jnp.float32))
            down_list.append(lax.dot_general(h, dz, (((0,), (0,)), ((), ())), preferred_element_type=jnp.float32))
    mixed = mixed_acc[:TOKENS].astype(jnp.bfloat16)
    input_grad = dx_acc[:TOKENS].astype(jnp.bfloat16)
    grad_gate = jnp.concatenate(gate_list, axis=1)
    grad_up = jnp.concatenate(up_list, axis=1)
    grad_down = jnp.concatenate(down_list, axis=0)
    return (mixed, input_grad, grad_gate, grad_up, grad_down)
```

```python
import functools

import jax
import jax.numpy as jnp
from jax import lax
from jax.experimental import pallas as pl
from jax.experimental.pallas import tpu as pltpu
from jax.sharding import PartitionSpec as P

EXPERTS = 8
CAP = 36
PIECE = 2 * CAP
MIB = 1 << 20
VMEM = pl.BlockSpec(memory_space=pltpu.VMEM)


def dot(left, right, dims=((1,), (0,))):
    return lax.dot_general(left, right, (dims, ((), ())), preferred_element_type=jnp.float32)


def params(mib):
    return pltpu.CompilerParams(vmem_limit_bytes=mib * MIB)


def cost(flops, moved):
    return pl.CostEstimate(flops=int(flops), bytes_accessed=int(moved), transcendentals=0)


def partner_expert(k, tiles):
    d = lax.axis_index("expert")
    return (2 * (lax.shift_right_logical(d, 1) ^ k) + (d & 1)) // tiles


def slot_rows(routing, chips, tiles):
    tok = routing.shape[1] // 2
    r0, r1, g0, g1 = (routing[i : i + 1, :] for i in range(4))
    before = (
        lax.broadcasted_iota(jnp.int32, (tok, tok), 0) < lax.broadcasted_iota(jnp.int32, (tok, tok), 1)
    ).astype(jnp.bfloat16)
    lane = lax.broadcasted_iota(jnp.int32, (1, 2 * tok), 1)
    base = jnp.where(lane >= tok, CAP, 0)
    result = []
    for k in range(chips):
        expert = partner_expert(k, tiles)
        first, second = r0 == expert, r1 == expert
        named = (first | second).astype(jnp.float32)
        flags = jnp.broadcast_to(named, (8, 2 * tok)).astype(jnp.bfloat16)
        position = jnp.concatenate(
            [dot(flags[:, :tok], before), dot(flags[:, tok:], before)], axis=1
        )[0:1]
        row = position.astype(jnp.int32) + base + k * PIECE
        gate = jnp.where(first, g0, g1)
        result.append((jnp.where(named > 0, row, -1), gate))
    return result


def dispatch_kernel(chips, tiles, scaled, routing_ref, other_routing_ref, own_ref, other_ref, *out_refs):
    tok, width = own_ref.shape
    routing = jnp.concatenate([routing_ref[...], other_routing_ref[...]], axis=1)
    slots = chips * PIECE
    row_id = lax.broadcasted_iota(jnp.int32, (slots, 2 * tok), 0)
    chosen = jnp.zeros((slots, 2 * tok), jnp.float32)
    factor = jnp.zeros((slots, 2 * tok), jnp.float32)
    for row, gate in slot_rows(routing, chips, tiles):
        hit = row_id == row
        chosen = jnp.where(hit, 1.0, chosen)
        if scaled:
            factor = jnp.where(hit, gate.astype(jnp.float32), factor)
    pick = chosen.astype(jnp.bfloat16)
    if scaled:
        scale = jnp.sum(factor, axis=1, keepdims=True) / 1024.0
    step = min(512, width)
    for col in range(0, width, step):
        rows = jnp.concatenate([own_ref[:, col : col + step], other_ref[:, col : col + step]], axis=0)
        moved = dot(pick, rows)
        if scaled:
            moved = scale * moved
        for k in range(chips):
            out_refs[k][:, col : col + step] = moved[k * PIECE : (k + 1) * PIECE].astype(jnp.bfloat16)


def dispatch(routing, other_routing, own, other, chips, tiles, scaled):
    width = own.shape[1]
    slots = chips * PIECE
    return pl.pallas_call(
        functools.partial(dispatch_kernel, chips, tiles, scaled),
        out_shape=[jax.ShapeDtypeStruct((PIECE, width), jnp.bfloat16)] * chips,
        in_specs=[VMEM] * 4,
        out_specs=[VMEM] * chips,
        compiler_params=params(24),
        cost_estimate=cost(4 * slots * own.shape[0] * width, 4 * (own.size + slots * width)),
        name="dispatch_dz" if scaled else "dispatch_x",
    )(routing, other_routing, own, other)


def combine_kernel(chips, tiles, scaled, routing_ref, other_routing_ref, *refs):
    backs, own_ref, other_ref = refs[:chips], refs[chips], refs[chips + 1]
    tok, width = own_ref.shape
    routing = jnp.concatenate([routing_ref[...], other_routing_ref[...]], axis=1)
    slots = chips * PIECE
    row_id = lax.broadcasted_iota(jnp.int32, (slots, 2 * tok), 0)
    high = jnp.zeros((slots, 2 * tok), jnp.float32)
    low = jnp.zeros((slots, 2 * tok), jnp.float32)
    for row, gate in slot_rows(routing, chips, tiles):
        hit = row_id == row
        if scaled:
            rest = gate & 3
            high = jnp.where(hit, (gate - rest).astype(jnp.float32), high)
            low = jnp.where(hit, rest.astype(jnp.float32), low)
        else:
            high = jnp.where(hit, 1.0, high)
    high = high.astype(jnp.bfloat16)
    low = low.astype(jnp.bfloat16)
    step = min(512, width)
    for col in range(0, width, step):
        rows = jnp.concatenate([back[:, col : col + step] for back in backs], axis=0)
        summed = dot(high, rows, ((0,), (0,)))
        if scaled:
            summed = (summed + dot(low, rows, ((0,), (0,)))) / 1024.0
        own_ref[:, col : col + step] = summed[:tok]
        other_ref[:, col : col + step] = summed[tok:]


def combine(routing, other_routing, backs, tiles, scaled):
    chips = len(backs)
    tok, width = routing.shape[1], backs[0].shape[1]
    return pl.pallas_call(
        functools.partial(combine_kernel, chips, tiles, scaled),
        out_shape=[jax.ShapeDtypeStruct((tok, width), jnp.float32)] * 2,
        in_specs=[VMEM] * (2 + chips),
        out_specs=[VMEM] * 2,
        compiler_params=params(24),
        cost_estimate=cost(4 * chips * PIECE * tok * width, 2 * chips * PIECE * width + 8 * tok * width),
        name="combine_mixed" if scaled else "combine_grad",
    )(routing, other_routing, *backs)


def forward_kernel(n, groups, *refs):
    pieces, (wg, wu, wd) = refs[:n], refs[n : n + 3]
    zs, a_ref, b_ref = refs[n + 3 : 2 * n + 3], refs[2 * n + 3], refs[2 * n + 4]
    sends = refs[2 * n + 5 : 2 * n + 5 + groups]
    x, total = refs[2 * n + 5 + groups :]
    step, last = pl.program_id(0), pl.num_programs(0) - 1
    share = x.shape[1] // groups
    tile = wg.shape[1]

    @pl.when(step == 0)
    def _():
        x[...] = jnp.concatenate([piece[...] for piece in pieces], axis=0)
        me = lax.axis_index("dp")
        for k in range(groups):
            start = pl.multiple_of((me ^ k) * share, share)
            sends[k][:, :share] = x[:, pl.ds(start, share)]

    a = dot(x[...], wg[...])
    b = dot(x[...], wu[...])
    h = (a * jax.nn.sigmoid(a) * b).astype(jnp.bfloat16)
    a_ref[...] = a
    b_ref[...] = b
    column = pl.multiple_of(share + step * tile, 128)
    for k in range(groups):
        sends[k][:, pl.ds(column, tile)] = h
    part = dot(h, wd[...])

    @pl.when(step == 0)
    def _():
        total[...] = part

    @pl.when(step > 0)
    def _():
        total[...] += part

    @pl.when(step == last)
    def _():
        for i in range(n):
            zs[i][...] = total[i * PIECE : (i + 1) * PIECE].astype(jnp.bfloat16)


def backward_kernel(n, groups, *refs):
    pieces, (a_ref, b_ref, wg, wu, wd) = refs[:n], refs[n : n + 5]
    dxs = refs[n + 5 : 2 * n + 5]
    sends = refs[2 * n + 5 : 2 * n + 5 + groups]
    dz, total = refs[2 * n + 5 + groups :]
    step, last = pl.program_id(0), pl.num_programs(0) - 1
    share = dz.shape[1] // groups
    tile = wg.shape[1]
    hidden = (sends[0].shape[1] - share) // 2

    @pl.when(step == 0)
    def _():
        dz[...] = jnp.concatenate([piece[...] for piece in pieces], axis=0)
        me = lax.axis_index("dp")
        for k in range(groups):
            start = pl.multiple_of((me ^ k) * share, share)
            sends[k][:, :share] = dz[:, pl.ds(start, share)]

    dh = dot(dz[...], wd[...], ((1,), (1,)))
    a, b = a_ref[...], b_ref[...]
    sig = jax.nn.sigmoid(a)
    d_gate = (dh * b * (sig * (1.0 + a * (1.0 - sig)))).astype(jnp.bfloat16)
    d_up = (dh * (a * sig)).astype(jnp.bfloat16)
    column = pl.multiple_of(share + step * tile, 128)
    for k in range(groups):
        sends[k][:, pl.ds(column, tile)] = d_gate
        sends[k][:, pl.ds(column + hidden, tile)] = d_up
    part = dot(d_gate, wg[...], ((1,), (1,))) + dot(d_up, wu[...], ((1,), (1,)))

    @pl.when(step == 0)
    def _():
        total[...] = part

    @pl.when(step > 0)
    def _():
        total[...] += part

    @pl.when(step == last)
    def _():
        for i in range(n):
            dxs[i][...] = total[i * PIECE : (i + 1) * PIECE].astype(jnp.bfloat16)


def whole(shape):
    return pl.BlockSpec(shape, lambda i: (0, 0))


def hidden_tile(hidden):
    return 256 if hidden % 256 == 0 else hidden


def forward(pieces, wg, wu, wd, groups):
    n = len(pieces)
    rows, width, hidden = n * PIECE, wg.shape[0], wg.shape[1]
    tile = hidden_tile(hidden)
    share = width // groups
    results = pl.pallas_call(
        functools.partial(forward_kernel, n, groups),
        grid=(hidden // tile,),
        out_shape=[jax.ShapeDtypeStruct((PIECE, width), jnp.bfloat16)] * n
        + [jax.ShapeDtypeStruct((rows, hidden), jnp.float32)] * 2
        + [jax.ShapeDtypeStruct((rows, share + hidden), jnp.bfloat16)] * groups,
        in_specs=[whole((PIECE, width))] * n
        + [pl.BlockSpec((width, tile), lambda i: (0, i))] * 2
        + [pl.BlockSpec((tile, width), lambda i: (i, 0))],
        out_specs=[whole((PIECE, width))] * n
        + [pl.BlockSpec((rows, tile), lambda i: (0, i))] * 2
        + [whole((rows, share + hidden))] * groups,
        scratch_shapes=[pltpu.VMEM((rows, width), jnp.bfloat16), pltpu.VMEM((rows, width), jnp.float32)],
        compiler_params=params(40),
        cost_estimate=cost(6 * rows * width * hidden, 6 * width * hidden + 8 * rows * width),
        name="experts_forward",
    )(*pieces, wg, wu, wd)
    return results[:n], results[n], results[n + 1], results[n + 2 :]


def backward(pieces, a, b, wg, wu, wd, groups):
    n = len(pieces)
    rows, width, hidden = n * PIECE, wg.shape[0], wg.shape[1]
    tile = hidden_tile(hidden)
    share = width // groups
    results = pl.pallas_call(
        functools.partial(backward_kernel, n, groups),
        grid=(hidden // tile,),
        out_shape=[jax.ShapeDtypeStruct((PIECE, width), jnp.bfloat16)] * n
        + [jax.ShapeDtypeStruct((rows, share + 2 * hidden), jnp.bfloat16)] * groups,
        in_specs=[whole((PIECE, width))] * n
        + [pl.BlockSpec((rows, tile), lambda i: (0, i))] * 2
        + [pl.BlockSpec((width, tile), lambda i: (0, i))] * 2
        + [pl.BlockSpec((tile, width), lambda i: (i, 0))],
        out_specs=[whole((PIECE, width))] * n + [whole((rows, share + 2 * hidden))] * groups,
        scratch_shapes=[pltpu.VMEM((rows, width), jnp.bfloat16), pltpu.VMEM((rows, width), jnp.float32)],
        compiler_params=params(40),
        cost_estimate=cost(6 * rows * width * hidden, 6 * width * hidden + 8 * rows * width),
        name="experts_backward",
    )(*pieces, a, b, wg, wu, wd)
    return results[:n], results[n:]


def weight_kernel(count, *refs):
    fwd, bwd = refs[:count], refs[count : 2 * count]
    gate_ref, up_ref, down_ref = refs[2 * count : 2 * count + 3]
    share, hidden = gate_ref.shape
    tile = min(256, hidden)
    x = jnp.concatenate([ref[:, :share] for ref in fwd], axis=0)
    dz = jnp.concatenate([ref[:, :share] for ref in bwd], axis=0)
    for col in range(0, hidden, tile):
        lo = share + col
        h = jnp.concatenate([ref[:, lo : lo + tile] for ref in fwd], axis=0)
        d_gate = jnp.concatenate([ref[:, lo : lo + tile] for ref in bwd], axis=0)
        d_up = jnp.concatenate([ref[:, lo + hidden : lo + hidden + tile] for ref in bwd], axis=0)
        gate_ref[:, col : col + tile] = dot(x, d_gate, ((0,), (0,)))
        up_ref[:, col : col + tile] = dot(x, d_up, ((0,), (0,)))
        down_ref[col : col + tile, :] = dot(h, dz, ((0,), (0,)))


def weight_grads(fwd, bwd, share, hidden):
    count = len(fwd)
    rows = sum(f.shape[0] for f in fwd)
    return pl.pallas_call(
        functools.partial(weight_kernel, count),
        out_shape=[jax.ShapeDtypeStruct((share, hidden), jnp.float32)] * 2
        + [jax.ShapeDtypeStruct((hidden, share), jnp.float32)],
        in_specs=[VMEM] * (2 * count),
        out_specs=[VMEM] * 3,
        compiler_params=params(56),
        cost_estimate=cost(6 * rows * share * hidden, 12 * share * hidden + 2 * rows * (2 * share + 3 * hidden)),
        name="weight_grads",
    )(*fwd, *bwd)


def per_device(tokens, routes, gates, cotangent, w_gate, w_up, w_down):
    devices, groups = lax.axis_size("expert"), lax.axis_size("dp")
    chips, tiles = devices // 2, devices // EXPERTS
    width, hidden = w_gate.shape
    share = width // groups

    def swap(v):
        return lax.ppermute(v, "expert", [(i, i ^ 1) for i in range(devices)])

    def over_z(v, k):
        return lax.ppermute(v, "expert", [(i, i ^ (2 * k)) for i in range(devices)]) if k else v

    def over_dp(v, k):
        return lax.ppermute(v, "dp", [(i, i ^ k) for i in range(groups)]) if k else v

    routing = jnp.concatenate([routes.T, gates.T], axis=0)
    other_routing = swap(routing)
    other_tokens = swap(tokens)
    other_cotangent = swap(cotangent)
    x_out = dispatch(routing, other_routing, tokens, other_tokens, chips, tiles, False)
    dz_out = dispatch(routing, other_routing, cotangent, other_cotangent, chips, tiles, True)
    half = chips // 2
    chunks = [list(range(half)), list(range(half, chips))]
    x_in, dz_in = {}, {}
    for k in reversed(range(chips)):
        x_in[k] = over_z(x_out[k], k)
    for k in reversed(range(chips)):
        dz_in[k] = over_z(dz_out[k], k)
    z_back, dx_back, fwd, bwd = {}, {}, [], []
    saved = []
    for chunk in chunks:
        zs, a, b, sends = forward([x_in[k] for k in chunk], w_gate, w_up, w_down, groups)
        saved.append((a, b))
        for k, z in zip(chunk, zs):
            z_back[k] = over_z(z, k)
        fwd += [over_dp(v, k) for k, v in enumerate(sends)]
    for chunk, (a, b) in zip(chunks, saved):
        dxs, sends = backward([dz_in[k] for k in chunk], a, b, w_gate, w_up, w_down, groups)
        for k, dx in zip(chunk, dxs):
            dx_back[k] = over_z(dx, k)
        bwd += [over_dp(v, k) for k, v in enumerate(sends)]

    def finish(back, scaled):
        mine, theirs = combine(routing, other_routing, [back[k] for k in range(chips)], tiles, scaled)
        return (mine + swap(theirs)).astype(jnp.bfloat16)

    mixed = finish(z_back, True)
    input_grad = finish(dx_back, False)
    grad_gate, grad_up, grad_down = weight_grads(fwd, bwd, share, hidden)
    return (mixed, input_grad, grad_gate, grad_up, grad_down)


def solution(mesh):
    rows = P(("dp", "expert"), None)
    in_specs = (rows, rows, rows, rows, P(None, "expert"), P(None, "expert"), P("expert", None))
    out_specs = (rows, rows, P("dp", "expert"), P("dp", "expert"), P("expert", "dp"))
    return jax.shard_map(
        per_device, mesh=mesh, in_specs=in_specs, out_specs=out_specs, check_vma=False
    )
```

```python
import functools

import jax
import jax.numpy as jnp
from jax import lax
from jax.experimental import pallas as pl
from jax.experimental.pallas import tpu as pltpu
from jax.sharding import PartitionSpec as P

EXPERTS = 8
CAP = 36
PIECE = 2 * CAP
KINDS = ("x", "dz")
MIB = 1 << 20
VMEM = pl.BlockSpec(memory_space=pltpu.VMEM)


def dot(left, right, dims=((1,), (0,))):
    return lax.dot_general(left, right, (dims, ((), ())), preferred_element_type=jnp.float32)


def params(mib):
    return pltpu.CompilerParams(vmem_limit_bytes=mib * MIB)


def cost(flops, moved):
    return pl.CostEstimate(flops=int(flops), bytes_accessed=int(moved), transcendentals=0)


def send_layout(groups, share, part, kinds):
    if groups != 4:
        return [(k, [(kind, k, 0, share) for kind in kinds] + [("part", 0, 0, part)]) for k in range(1, groups)], 0
    half, cut = part // 2, share // 2
    left, right = ("part", 0, 0, half), ("part", 0, half, half)
    over_x = [(kind, 1, 0, share) for kind in kinds] + [right, left] + [(kind, 3, 0, cut) for kind in kinds]
    over_y = [(kind, 2, 0, share) for kind in kinds] + [left, right] + [(kind, 3, cut, cut) for kind in kinds]
    return [(1, over_x), (2, over_y)], half + cut * len(kinds)


def own_fields(share, part, kinds):
    return [(kind, 0, 0, share) for kind in kinds] + [("part", 0, 0, part)]


def all_layouts(groups, share, part, kinds):
    return [own_fields(share, part, kinds)] + [f for _, f in send_layout(groups, share, part, kinds)[0]]


def fields_width(fields):
    return sum(field[3] for field in fields)


def received(groups, share, part, kinds):
    messages, relayed = send_layout(groups, share, part, kinds)
    result = []
    for index, (sent, fields) in enumerate([(0, own_fields(share, part, kinds))] + messages):
        column, found = 0, {}
        for kind, offset, first, count in fields:
            if kind == "part" or offset == sent:
                found.setdefault(kind, []).append((index, column, first, count))
            column += count
        found["part"].sort(key=lambda f: f[2])
        result.append(found)
    if relayed:
        half, cut = part // 2, share // 2
        found = {"part": [(3, 0, 0, half), (4, 0, half, half)]}
        for i, kind in enumerate(kinds):
            found[kind] = [(3, half + i * cut, 0, cut), (4, half + i * cut, cut, cut)]
        result.append(found)
    return result


def store_rows(outs, layouts, want, source, top, share):
    me = lax.axis_index("dp")
    for out, fields in zip(outs, layouts):
        column = 0
        for kind, offset, first, count in fields:
            if kind == want:
                start = pl.multiple_of((me ^ offset) * share + first, 128)
                out[:, column : column + count] = source[top : top + PIECE, pl.ds(start, count)]
            column += count


def store_part(outs, layouts, step, tile, value, base=0):
    for out, fields in zip(outs, layouts):
        column = 0
        for kind, _, first, count in fields:
            if kind == "part":
                at = base + step * tile - first

                @pl.when((at >= 0) & (at < count))
                def _(out=out, column=column, at=at):
                    out[:, pl.ds(pl.multiple_of(column + at, 128), tile)] = value

            column += count


def partner_expert(k, tiles):
    d = lax.axis_index("expert")
    return (2 * (lax.shift_right_logical(d, 1) ^ k) + (d & 1)) // tiles


def slot_rows(routing, chips, tiles):
    tok = routing.shape[1] // 2
    r0, r1, g0, g1 = (routing[i : i + 1, :] for i in range(4))
    before = (
        lax.broadcasted_iota(jnp.int32, (tok, tok), 0) < lax.broadcasted_iota(jnp.int32, (tok, tok), 1)
    ).astype(jnp.bfloat16)
    lane = lax.broadcasted_iota(jnp.int32, (1, 2 * tok), 1)
    base = jnp.where(lane >= tok, CAP, 0)
    result = []
    for k in range(chips):
        expert = partner_expert(k, tiles)
        first, second = r0 == expert, r1 == expert
        named = (first | second).astype(jnp.float32)
        flags = jnp.broadcast_to(named, (8, 2 * tok)).astype(jnp.bfloat16)
        position = jnp.concatenate(
            [dot(flags[:, :tok], before), dot(flags[:, tok:], before)], axis=1
        )[0:1]
        row = position.astype(jnp.int32) + base + k * PIECE
        gate = jnp.where(first, g0, g1)
        result.append((jnp.where(named > 0, row, -1), gate))
    return result


def dispatch_kernel(chips, tiles, routing_ref, other_routing_ref, x_ref, other_x_ref, dy_ref, other_dy_ref, *out_refs):
    tok, width = x_ref.shape
    routing = jnp.concatenate([routing_ref[...], other_routing_ref[...]], axis=1)
    slots = chips * PIECE
    row_id = lax.broadcasted_iota(jnp.int32, (slots, 2 * tok), 0)
    chosen = jnp.zeros((slots, 2 * tok), jnp.float32)
    factor = jnp.zeros((slots, 2 * tok), jnp.float32)
    for row, gate in slot_rows(routing, chips, tiles):
        hit = row_id == row
        chosen = jnp.where(hit, 1.0, chosen)
        factor = jnp.where(hit, gate.astype(jnp.float32), factor)
    pick = chosen.astype(jnp.bfloat16)
    scale = jnp.sum(factor, axis=1, keepdims=True) / 1024.0
    step = min(512, width)
    for col in range(0, width, step):
        columns = slice(col, col + step)
        x = dot(pick, jnp.concatenate([x_ref[:, columns], other_x_ref[:, columns]], axis=0))
        dz = scale * dot(pick, jnp.concatenate([dy_ref[:, columns], other_dy_ref[:, columns]], axis=0))
        for k in range(chips):
            rows = slice(k * PIECE, (k + 1) * PIECE)
            out_refs[k][:, columns] = jnp.concatenate([x[rows], dz[rows]], axis=0).astype(jnp.bfloat16)


def dispatch(routing, other_routing, x, other_x, dy, other_dy, chips, tiles):
    tok, width = x.shape
    slots = chips * PIECE
    return pl.pallas_call(
        functools.partial(dispatch_kernel, chips, tiles),
        out_shape=[jax.ShapeDtypeStruct((2 * PIECE, width), jnp.bfloat16)] * chips,
        in_specs=[VMEM] * 6,
        out_specs=[VMEM] * chips,
        compiler_params=params(24),
        cost_estimate=cost(8 * slots * tok * width, 4 * (2 * x.size + slots * width)),
        name="dispatch",
    )(routing, other_routing, *in_hbm(x), other_x, *in_hbm(dy), other_dy)


def combine_kernel(chips, tiles, scaled, routing_ref, other_routing_ref, *refs):
    backs, own_ref, other_ref = refs[:chips], refs[chips], refs[chips + 1]
    tok, width = own_ref.shape
    routing = jnp.concatenate([routing_ref[...], other_routing_ref[...]], axis=1)
    slots = chips * PIECE
    row_id = lax.broadcasted_iota(jnp.int32, (slots, 2 * tok), 0)
    high = jnp.zeros((slots, 2 * tok), jnp.float32)
    low = jnp.zeros((slots, 2 * tok), jnp.float32)
    for row, gate in slot_rows(routing, chips, tiles):
        hit = row_id == row
        if scaled:
            rest = gate & 3
            high = jnp.where(hit, (gate - rest).astype(jnp.float32), high)
            low = jnp.where(hit, rest.astype(jnp.float32), low)
        else:
            high = jnp.where(hit, 1.0, high)
    high = high.astype(jnp.bfloat16)
    low = low.astype(jnp.bfloat16)
    step, lo = min(512, width), 0 if scaled else PIECE
    for col in range(0, width, step):
        rows = jnp.concatenate([back[lo : lo + PIECE, col : col + step] for back in backs], axis=0)
        summed = dot(high, rows, ((0,), (0,)))
        if scaled:
            summed = (summed + dot(low, rows, ((0,), (0,)))) / 1024.0
        own_ref[:, col : col + step] = summed[:tok]
        other_ref[:, col : col + step] = summed[tok:]


def combine(routing, other_routing, backs, tiles, scaled):
    chips = len(backs)
    tok, width = routing.shape[1], backs[0].shape[1]
    return pl.pallas_call(
        functools.partial(combine_kernel, chips, tiles, scaled),
        out_shape=[jax.ShapeDtypeStruct((tok, width), jnp.float32)] * 2,
        in_specs=[VMEM] * (2 + chips),
        out_specs=[VMEM] * 2,
        compiler_params=params(24),
        cost_estimate=cost(4 * chips * PIECE * tok * width, 2 * chips * PIECE * width + 8 * tok * width),
        name="combine_mixed" if scaled else "combine_grad",
    )(routing, other_routing, *backs)


def add_to(total, part, step):
    @pl.when(step == 0)
    def _():
        total[...] = part

    @pl.when(step > 0)
    def _():
        total[...] += part


def experts_kernel(layouts, share, hidden, rows_ref, wg, wu, wd, back_ref, *refs):
    sends, (z_total, dx_total) = refs[: len(layouts)], refs[len(layouts) :]
    step, last = pl.program_id(0), pl.num_programs(0) - 1
    tile = wg.shape[1]

    @pl.when(step == 0)
    def _():
        store_rows(sends, layouts, "x", rows_ref, 0, share)
        store_rows(sends, layouts, "dz", rows_ref, PIECE, share)

    x, dz = rows_ref[:PIECE, :], rows_ref[PIECE:, :]
    a, b = dot(x, wg[...]), dot(x, wu[...])
    dh = dot(dz, wd[...], ((1,), (1,)))
    sig = jax.nn.sigmoid(a)
    act = a * sig
    h = (act * b).astype(jnp.bfloat16)
    d_gate = (dh * b * (sig * (1.0 + a * (1.0 - sig)))).astype(jnp.bfloat16)
    d_up = (dh * act).astype(jnp.bfloat16)
    store_part(sends, layouts, step, tile, h, 0)
    store_part(sends, layouts, step, tile, d_gate, hidden)
    store_part(sends, layouts, step, tile, d_up, 2 * hidden)
    add_to(z_total, dot(h, wd[...]), step)
    add_to(dx_total, dot(d_gate, wg[...], ((1,), (1,))) + dot(d_up, wu[...], ((1,), (1,))), step)

    @pl.when(step == last)
    def _():
        back_ref[...] = jnp.concatenate([z_total[...], dx_total[...]], axis=0).astype(jnp.bfloat16)


def whole(shape):
    return pl.BlockSpec(shape, lambda i: (0, 0))


def in_hbm(*weights):
    return [pltpu.with_memory_space_constraint(w, pltpu.HBM) for w in weights]


def hidden_tile(hidden):
    return 256 if hidden % 256 == 0 else hidden


def experts(rows, weights, groups):
    width, hidden = weights[0].shape
    tile, share = hidden_tile(hidden), width // groups
    layouts = all_layouts(groups, share, 3 * hidden, KINDS)
    sends = [(PIECE, fields_width(fields)) for fields in layouts]
    columns = pl.BlockSpec((width, tile), lambda i: (0, i))
    results = pl.pallas_call(
        functools.partial(experts_kernel, layouts, share, hidden),
        grid=(hidden // tile,),
        out_shape=[jax.ShapeDtypeStruct((2 * PIECE, width), jnp.bfloat16)]
        + [jax.ShapeDtypeStruct(shape, jnp.bfloat16) for shape in sends],
        in_specs=[whole((2 * PIECE, width)), columns, columns, pl.BlockSpec((tile, width), lambda i: (i, 0))],
        out_specs=[whole((2 * PIECE, width))] + [whole(shape) for shape in sends],
        scratch_shapes=[pltpu.VMEM((PIECE, width), jnp.float32)] * 2,
        compiler_params=params(24),
        cost_estimate=cost(12 * PIECE * width * hidden, 6 * width * hidden + 8 * PIECE * width),
        name="experts",
    )(rows, *in_hbm(*weights))
    return results[0], list(results[1:])


def take(refs, fields):
    return jnp.concatenate([refs[i][:, column : column + count] for i, column, _, count in fields], axis=1)


def take_tile(refs, fields, lo, tile):
    for i, column, first, count in fields:
        if first <= lo < first + count:
            return refs[i][:, column + lo - first : column + lo - first + tile]


def weight_kernel(groups, count, *refs):
    gate_ref, up_ref, down_ref = refs[-3:]
    share, hidden = gate_ref.shape
    tile = min(256, hidden)
    fields = received(groups, share, 3 * hidden, KINDS)
    sources = [(refs[at : at + count], found) for at in range(0, len(refs) - 3, count) for found in fields]
    x = jnp.concatenate([take(arrays, found["x"]) for arrays, found in sources], axis=0)
    dz = jnp.concatenate([take(arrays, found["dz"]) for arrays, found in sources], axis=0)

    def part(lo):
        return jnp.concatenate([take_tile(arrays, found["part"], lo, tile) for arrays, found in sources], axis=0)

    for col in range(0, hidden, tile):
        gate_ref[:, col : col + tile] = dot(x, part(hidden + col), ((0,), (0,)))
        up_ref[:, col : col + tile] = dot(x, part(2 * hidden + col), ((0,), (0,)))
        down_ref[col : col + tile, :] = dot(part(col), dz, ((0,), (0,)))


def weight_grads(sets, groups, share, hidden):
    arrays = [array for one in sets for array in one]
    rows = groups * len(sets) * PIECE
    return pl.pallas_call(
        functools.partial(weight_kernel, groups, len(sets[0])),
        out_shape=[jax.ShapeDtypeStruct((share, hidden), jnp.float32)] * 2
        + [jax.ShapeDtypeStruct((hidden, share), jnp.float32)],
        in_specs=[VMEM] * len(arrays),
        out_specs=[VMEM] * 3,
        compiler_params=params(48),
        cost_estimate=cost(6 * rows * share * hidden, 12 * share * hidden + 2 * rows * (2 * share + 3 * hidden)),
        name="weight_grads",
    )(*arrays)


def per_device(tokens, routes, gates, cotangent, w_gate, w_up, w_down):
    devices, groups = lax.axis_size("expert"), lax.axis_size("dp")
    chips, tiles = devices // 2, devices // EXPERTS
    width, hidden = w_gate.shape
    share = width // groups

    def swap(v):
        return lax.ppermute(v, "expert", [(i, i ^ 1) for i in range(devices)])

    def over_z(v, k):
        return lax.ppermute(v, "expert", [(i, i ^ (2 * k)) for i in range(devices)]) if k else v

    def over_dp(v, k):
        return lax.ppermute(v, "dp", [(i, i ^ k) for i in range(groups)]) if k else v

    def after(values, *others):
        return lax.optimization_barrier((values, others))[0]

    messages, relayed = send_layout(groups, share, 3 * hidden, KINDS)

    def first_phase(sends):
        return [sends[0]] + [over_dp(v, k) for v, (k, _) in zip(sends[1:], messages)]

    def second_phase(first, second):
        if relayed:
            for index, k in ((1, 2), (2, 1)):
                both = jnp.concatenate([first[index][:, -relayed:], second[index][:, -relayed:]], axis=0)
                both = over_dp(both, k)
                first.append(both[:PIECE])
                second.append(both[PIECE:])
        return first, second

    routing = jnp.concatenate([routes.T, gates.T], axis=0)
    other_routing = swap(routing)
    out = dispatch(routing, other_routing, tokens, swap(tokens), cotangent, swap(cotangent), chips, tiles)
    weights = (w_gate, w_up, w_down)
    order = [0, 1] + list(range(chips - 1, 1, -1))
    rows = {k: over_z(out[k], k) for k in order}
    back, sets, previous = {}, [], []
    last = order[-1]
    for k in order[:-1]:
        back[k], sends = experts(after(rows[k], *previous), weights, groups)
        if len(sets) == 2:
            sends = after(sends, *sets[0])
        sets.append(first_phase(sends))
        previous = [back[k]]
    held = after([back[k] for k in order[:-1]], back[order[-2]])
    back.update(zip(order[:-1], held))
    got = {k: over_z(back[k], k) for k in order[2:-1]}
    back[last], sends = experts(after(rows[last], *previous, *sets[0], *sets[1]), weights, groups)
    got[last] = over_z(back[last], last)
    got[0], got[1] = back[0], over_z(back[1], 1)
    sends = after(sends, *sets[2], got[1])
    sets.append(first_phase(sends))
    sets[0], sets[1] = after((sets[0], sets[1]), back[last])
    sets[:2] = second_phase(*sets[:2])
    sets[2:4] = second_phase(*sets[2:4])
    grads = weight_grads(sets, groups, share, hidden)
    back = after([got[k] for k in range(chips)], *grads)

    def finish(scaled):
        mine, theirs = combine(routing, other_routing, back, tiles, scaled)
        return (mine + swap(theirs)).astype(jnp.bfloat16)

    mixed, input_grad = finish(True), finish(False)
    return (mixed, input_grad, *grads)


def solution(mesh):
    rows = P(("dp", "expert"), None)
    in_specs = (rows, rows, rows, rows, P(None, "expert"), P(None, "expert"), P("expert", None))
    out_specs = (rows, rows, P("dp", "expert"), P("dp", "expert"), P("expert", "dp"))
    return jax.shard_map(
        per_device, mesh=mesh, in_specs=in_specs, out_specs=out_specs, check_vma=False
    )
```

```python
import functools

import jax
import jax.numpy as jnp
from jax import lax
from jax.experimental import pallas as pl
from jax.experimental.pallas import tpu as pltpu
from jax.sharding import PartitionSpec as P

EXPERTS = 8
CAP = 36
PIECE = 2 * CAP
KINDS = ("x", "dz")
MIB = 1 << 20
VMEM = pl.BlockSpec(memory_space=pltpu.VMEM)


def dot(left, right, dims=((1,), (0,))):
    return lax.dot_general(left, right, (dims, ((), ())), preferred_element_type=jnp.float32)


def params(mib):
    return pltpu.CompilerParams(vmem_limit_bytes=mib * MIB)


def cost(flops, moved):
    return pl.CostEstimate(flops=int(flops), bytes_accessed=int(moved), transcendentals=0)


def send_layout(groups, share, part, kinds):
    if groups != 4:
        return [(k, [(kind, k, 0, share) for kind in kinds] + [("part", 0, 0, part)]) for k in range(1, groups)], 0
    half, cut = part // 2, share // 2
    left, right = ("part", 0, 0, half), ("part", 0, half, half)
    over_x = [(kind, 1, 0, share) for kind in kinds] + [right, left] + [(kind, 3, 0, cut) for kind in kinds]
    over_y = [(kind, 2, 0, share) for kind in kinds] + [left, right] + [(kind, 3, cut, cut) for kind in kinds]
    return [(1, over_x), (2, over_y)], half + cut * len(kinds)


def own_fields(share, part, kinds):
    return [(kind, 0, 0, share) for kind in kinds] + [("part", 0, 0, part)]


def all_layouts(groups, share, part, kinds):
    return [own_fields(share, part, kinds)] + [f for _, f in send_layout(groups, share, part, kinds)[0]]


def fields_width(fields):
    return sum(field[3] for field in fields)


def received(groups, share, part, kinds):
    messages, relayed = send_layout(groups, share, part, kinds)
    result = []
    for index, (sent, fields) in enumerate([(0, own_fields(share, part, kinds))] + messages):
        column, found = 0, {}
        for kind, offset, first, count in fields:
            if kind == "part" or offset == sent:
                found.setdefault(kind, []).append((index, column, first, count))
            column += count
        found["part"].sort(key=lambda f: f[2])
        result.append(found)
    if relayed:
        half, cut = part // 2, share // 2
        found = {"part": [(3, 0, 0, half), (4, 0, half, half)]}
        for i, kind in enumerate(kinds):
            found[kind] = [(3, half + i * cut, 0, cut), (4, half + i * cut, cut, cut)]
        result.append(found)
    return result


def store_rows(outs, layouts, want, source, top, share):
    me = lax.axis_index("dp")
    for out, fields in zip(outs, layouts):
        column = 0
        for kind, offset, first, count in fields:
            if kind == want:
                start = pl.multiple_of((me ^ offset) * share + first, 128)
                out[:, column : column + count] = source[top : top + PIECE, pl.ds(start, count)]
            column += count


def store_part(outs, layouts, step, tile, value, base=0):
    for out, fields in zip(outs, layouts):
        column = 0
        for kind, _, first, count in fields:
            if kind == "part":
                at = base + step * tile - first

                @pl.when((at >= 0) & (at < count))
                def _(out=out, column=column, at=at):
                    out[:, pl.ds(pl.multiple_of(column + at, 128), tile)] = value

            column += count


def partner_expert(k, tiles):
    d = lax.axis_index("expert")
    return (2 * (lax.shift_right_logical(d, 1) ^ k) + (d & 1)) // tiles


def slot_rows(routing, chips, tiles):
    tok = routing.shape[1] // 2
    r0, r1, g0, g1 = (routing[i : i + 1, :] for i in range(4))
    before = (
        lax.broadcasted_iota(jnp.int32, (tok, tok), 0) < lax.broadcasted_iota(jnp.int32, (tok, tok), 1)
    ).astype(jnp.bfloat16)
    lane = lax.broadcasted_iota(jnp.int32, (1, 2 * tok), 1)
    base = jnp.where(lane >= tok, CAP, 0)
    result = []
    for k in range(chips):
        expert = partner_expert(k, tiles)
        first, second = r0 == expert, r1 == expert
        named = (first | second).astype(jnp.float32)
        flags = jnp.broadcast_to(named, (8, 2 * tok)).astype(jnp.bfloat16)
        position = jnp.concatenate(
            [dot(flags[:, :tok], before), dot(flags[:, tok:], before)], axis=1
        )[0:1]
        row = position.astype(jnp.int32) + base + k * PIECE
        gate = jnp.where(first, g0, g1)
        result.append((jnp.where(named > 0, row, -1), gate))
    return result


def dispatch_kernel(chips, tiles, routing_ref, other_routing_ref, x_ref, other_x_ref, dy_ref, other_dy_ref, *out_refs):
    tok, width = x_ref.shape
    routing = jnp.concatenate([routing_ref[...], other_routing_ref[...]], axis=1)
    slots = chips * PIECE
    row_id = lax.broadcasted_iota(jnp.int32, (slots, 2 * tok), 0)
    chosen = jnp.zeros((slots, 2 * tok), jnp.float32)
    factor = jnp.zeros((slots, 2 * tok), jnp.float32)
    for row, gate in slot_rows(routing, chips, tiles):
        hit = row_id == row
        chosen = jnp.where(hit, 1.0, chosen)
        factor = jnp.where(hit, gate.astype(jnp.float32), factor)
    pick = chosen.astype(jnp.bfloat16)
    scale = jnp.sum(factor, axis=1, keepdims=True) / 1024.0
    step = min(512, width)
    for col in range(0, width, step):
        columns = slice(col, col + step)
        x = dot(pick, jnp.concatenate([x_ref[:, columns], other_x_ref[:, columns]], axis=0))
        dz = scale * dot(pick, jnp.concatenate([dy_ref[:, columns], other_dy_ref[:, columns]], axis=0))
        for k in range(chips):
            rows = slice(k * PIECE, (k + 1) * PIECE)
            out_refs[k][:, columns] = jnp.concatenate([x[rows], dz[rows]], axis=0).astype(jnp.bfloat16)


def dispatch(routing, other_routing, x, other_x, dy, other_dy, chips, tiles):
    tok, width = x.shape
    slots = chips * PIECE
    return pl.pallas_call(
        functools.partial(dispatch_kernel, chips, tiles),
        out_shape=[jax.ShapeDtypeStruct((2 * PIECE, width), jnp.bfloat16)] * chips,
        in_specs=[VMEM] * 6,
        out_specs=[VMEM] * chips,
        compiler_params=params(24),
        cost_estimate=cost(8 * slots * tok * width, 4 * (2 * x.size + slots * width)),
        name="dispatch",
    )(routing, other_routing, *in_hbm(x), other_x, *in_hbm(dy), other_dy)


def combine_kernel(chips, tiles, scaled, routing_ref, other_routing_ref, *refs):
    backs, own_ref, other_ref = refs[:chips], refs[chips], refs[chips + 1]
    tok, width = own_ref.shape
    routing = jnp.concatenate([routing_ref[...], other_routing_ref[...]], axis=1)
    slots = chips * PIECE
    row_id = lax.broadcasted_iota(jnp.int32, (slots, 2 * tok), 0)
    high = jnp.zeros((slots, 2 * tok), jnp.float32)
    low = jnp.zeros((slots, 2 * tok), jnp.float32)
    for row, gate in slot_rows(routing, chips, tiles):
        hit = row_id == row
        if scaled:
            rest = gate & 3
            high = jnp.where(hit, (gate - rest).astype(jnp.float32), high)
            low = jnp.where(hit, rest.astype(jnp.float32), low)
        else:
            high = jnp.where(hit, 1.0, high)
    high = high.astype(jnp.bfloat16)
    low = low.astype(jnp.bfloat16)
    step, lo = min(512, width), 0 if scaled else PIECE
    for col in range(0, width, step):
        rows = jnp.concatenate([back[lo : lo + PIECE, col : col + step] for back in backs], axis=0)
        summed = dot(high, rows, ((0,), (0,)))
        if scaled:
            summed = (summed + dot(low, rows, ((0,), (0,)))) / 1024.0
        own_ref[:, col : col + step] = summed[:tok]
        other_ref[:, col : col + step] = summed[tok:]


def combine(routing, other_routing, backs, tiles, scaled):
    chips = len(backs)
    tok, width = routing.shape[1], backs[0].shape[1]
    return pl.pallas_call(
        functools.partial(combine_kernel, chips, tiles, scaled),
        out_shape=[jax.ShapeDtypeStruct((tok, width), jnp.float32)] * 2,
        in_specs=[VMEM] * (2 + chips),
        out_specs=[VMEM] * 2,
        compiler_params=params(24),
        cost_estimate=cost(4 * chips * PIECE * tok * width, 2 * chips * PIECE * width + 8 * tok * width),
        name="combine_mixed" if scaled else "combine_grad",
    )(routing, other_routing, *backs)


def add_to(total, part, step):
    @pl.when(step == 0)
    def _():
        total[...] = part

    @pl.when(step > 0)
    def _():
        total[...] += part


def experts_kernel(layouts, share, hidden, rows_ref, wg, wu, wd, back_ref, *refs):
    sends, (z_total, dx_total) = refs[: len(layouts)], refs[len(layouts) :]
    step, last = pl.program_id(0), pl.num_programs(0) - 1
    tile = wg.shape[1]

    @pl.when(step == 0)
    def _():
        store_rows(sends, layouts, "x", rows_ref, 0, share)
        store_rows(sends, layouts, "dz", rows_ref, PIECE, share)

    x, dz = rows_ref[:PIECE, :], rows_ref[PIECE:, :]
    a, b = dot(x, wg[...]), dot(x, wu[...])
    dh = dot(dz, wd[...], ((1,), (1,)))
    sig = jax.nn.sigmoid(a)
    act = a * sig
    h = (act * b).astype(jnp.bfloat16)
    d_gate = (dh * b * (sig * (1.0 + a * (1.0 - sig)))).astype(jnp.bfloat16)
    d_up = (dh * act).astype(jnp.bfloat16)
    store_part(sends, layouts, step, tile, h, 0)
    store_part(sends, layouts, step, tile, d_gate, hidden)
    store_part(sends, layouts, step, tile, d_up, 2 * hidden)
    add_to(z_total, dot(h, wd[...]), step)
    add_to(dx_total, dot(d_gate, wg[...], ((1,), (1,))) + dot(d_up, wu[...], ((1,), (1,))), step)

    @pl.when(step == last)
    def _():
        back_ref[...] = jnp.concatenate([z_total[...], dx_total[...]], axis=0).astype(jnp.bfloat16)


def whole(shape):
    return pl.BlockSpec(shape, lambda i: (0, 0))


def in_hbm(*weights):
    return [pltpu.with_memory_space_constraint(w, pltpu.HBM) for w in weights]


def hidden_tile(hidden):
    return 512 if hidden % 512 == 0 else hidden


def experts(rows, weights, groups):
    width, hidden = weights[0].shape
    tile, share = hidden_tile(hidden), width // groups
    layouts = all_layouts(groups, share, 3 * hidden, KINDS)
    sends = [(PIECE, fields_width(fields)) for fields in layouts]
    columns = pl.BlockSpec((width, tile), lambda i: (0, i))
    results = pl.pallas_call(
        functools.partial(experts_kernel, layouts, share, hidden),
        grid=(hidden // tile,),
        out_shape=[jax.ShapeDtypeStruct((2 * PIECE, width), jnp.bfloat16)]
        + [jax.ShapeDtypeStruct(shape, jnp.bfloat16) for shape in sends],
        in_specs=[whole((2 * PIECE, width)), columns, columns, pl.BlockSpec((tile, width), lambda i: (i, 0))],
        out_specs=[whole((2 * PIECE, width))] + [whole(shape) for shape in sends],
        scratch_shapes=[pltpu.VMEM((PIECE, width), jnp.float32)] * 2,
        compiler_params=params(28),
        cost_estimate=cost(12 * PIECE * width * hidden, 6 * width * hidden),
        name="experts",
    )(rows, *in_hbm(*weights))
    return results[0], list(results[1:])


def take(refs, fields):
    return jnp.concatenate([refs[i][:, column : column + count] for i, column, _, count in fields], axis=1)


def take_tile(refs, fields, lo, tile):
    for i, column, first, count in fields:
        if first <= lo < first + count:
            return refs[i][:, column + lo - first : column + lo - first + tile]


def weight_kernel(plan, partial, final, *refs):
    count = len(refs) - (7 if final else 3)
    arrays, outs = refs[:count], refs[count : count + 3]
    results, sems = (refs[count + 3 : count + 6], refs[count + 6]) if final else (outs, None)
    share, hidden = results[0].shape
    tile = min(256, hidden)
    x = jnp.concatenate([take(arrays, found["x"]) for found in plan], axis=0)
    dz = jnp.concatenate([take(arrays, found["dz"]) for found in plan], axis=0)
    copies = []

    def part(lo):
        return jnp.concatenate([take_tile(arrays, found["part"], lo, tile) for found in plan], axis=0)

    def put(which, rows, columns, left, right):
        value = dot(left, right, ((0,), (0,)))
        if partial:
            value = value + arrays[which][rows, columns]
        results[which][rows, columns] = value
        if final:
            to = outs[which].at[rows, columns]
            copies.append(pltpu.make_async_copy(results[which].at[rows, columns], to, sems.at[len(copies)]))
            copies[-1].start()

    for col in range(0, hidden, tile):
        part_of, whole_of = pl.ds(col, tile), pl.ds(0, share)
        put(0, whole_of, part_of, x, part(hidden + col))
        put(1, whole_of, part_of, x, part(2 * hidden + col))
        put(2, part_of, whole_of, part(col), dz)
    for copy in copies:
        copy.wait()


def weight_grads(sources, partial, final, share, hidden):
    arrays, plan = list(partial), []
    for have, found in sources:
        used = sorted({field[0] for fields in found.values() for field in fields})
        at = {index: len(arrays) + i for i, index in enumerate(used)}
        arrays += [have[index] for index in used]
        plan.append({kind: [(at[f[0]], *f[1:]) for f in fields] for kind, fields in found.items()})
    rows = len(sources) * PIECE
    shapes = [(share, hidden), (share, hidden), (hidden, share)]
    scratch = [pltpu.VMEM(shape, jnp.float32) for shape in shapes]
    scratch += [pltpu.SemaphoreType.DMA((3 * hidden // min(256, hidden),))]
    return pl.pallas_call(
        functools.partial(weight_kernel, plan, bool(partial), final),
        out_shape=[jax.ShapeDtypeStruct(shape, jnp.float32) for shape in shapes],
        in_specs=[VMEM] * len(arrays),
        out_specs=[pl.BlockSpec(memory_space=pl.ANY) if final else VMEM] * 3,
        scratch_shapes=scratch if final else [],
        compiler_params=params(48),
        cost_estimate=cost(6 * rows * share * hidden, 12 * share * hidden + 2 * rows * (2 * share + 3 * hidden)),
        name="weight_grads" if final else "weight_grads_early",
    )(*arrays)


def per_device(tokens, routes, gates, cotangent, w_gate, w_up, w_down):
    devices, groups = lax.axis_size("expert"), lax.axis_size("dp")
    chips, tiles = devices // 2, devices // EXPERTS
    width, hidden = w_gate.shape
    share = width // groups

    def swap(v):
        return lax.ppermute(v, "expert", [(i, i ^ 1) for i in range(devices)])

    def over_z(v, k):
        return lax.ppermute(v, "expert", [(i, i ^ (2 * k)) for i in range(devices)]) if k else v

    def over_dp(v, k):
        return lax.ppermute(v, "dp", [(i, i ^ k) for i in range(groups)]) if k else v

    def after(values, *others):
        return lax.optimization_barrier((values, others))[0]

    messages, relayed = send_layout(groups, share, 3 * hidden, KINDS)

    def first_phase(sends):
        return [sends[0]] + [over_dp(v, k) for v, (k, _) in zip(sends[1:], messages)]

    def second_phase(first, second):
        if relayed:
            for index, k in ((1, 2), (2, 1)):
                both = jnp.concatenate([first[index][:, -relayed:], second[index][:, -relayed:]], axis=0)
                both = over_dp(both, k)
                first.append(both[:PIECE])
                second.append(both[PIECE:])
        return first, second

    routing = jnp.concatenate([routes.T, gates.T], axis=0)
    other_routing = swap(routing)
    out = dispatch(routing, other_routing, tokens, swap(tokens), cotangent, swap(cotangent), chips, tiles)
    weights = (w_gate, w_up, w_down)
    order = [0, 1] + list(range(chips - 1, 1, -1))
    rows = {k: over_z(out[k], k) for k in order}
    back, sets, previous = {}, [], []
    last, early = order[-1], order[-2]
    for k in order[:-1]:
        back[k], sends = experts(after(rows[k], *previous), weights, groups)
        if len(sets) == 2:
            sends = after(sends, *sets[0])
        sets.append(first_phase(sends))
        previous = [back[k]]
    back[1] = after(back[1], back[early])
    got = {0: back[0]}
    got[1] = over_z(back[1], 1)
    got.update({k: over_z(back[k], k) for k in order[1:-1] if k != 1})
    back[last], sends = experts(after(rows[last], *previous, *sets[0], *sets[1]), weights, groups)
    back[last] = after(back[last], got[1])
    got[last] = over_z(back[last], last)
    sets[:2] = second_phase(*sets[:2])
    sends = after(sends, *sets[2])
    sets.append(first_phase(sends))
    sets[2:4] = second_phase(*sets[2:4])
    fields = received(groups, share, 3 * hidden, KINDS)
    sources = [(one, found) for one in sets for found in fields]
    cut = (len(sets) - 2) * len(fields) + (len(fields) - 1) * 1
    early_grads = weight_grads(sources[:cut], [], False, share, hidden)
    grads = weight_grads(sources[cut:], early_grads, True, share, hidden)
    back = after([got[k] for k in range(chips)], *grads)

    def finish(scaled):
        mine, theirs = combine(routing, other_routing, back, tiles, scaled)
        return (mine + swap(theirs)).astype(jnp.bfloat16)

    mixed, input_grad = finish(True), finish(False)
    return (mixed, input_grad, *grads)


def solution(mesh):
    rows = P(("dp", "expert"), None)
    in_specs = (rows, rows, rows, rows, P(None, "expert"), P(None, "expert"), P("expert", None))
    out_specs = (rows, rows, P("dp", "expert"), P("dp", "expert"), P("expert", "dp"))
    return jax.shard_map(
        per_device, mesh=mesh, in_specs=in_specs, out_specs=out_specs, check_vma=False
    )
```

```python
import functools

import jax
import jax.numpy as jnp
from jax import lax
from jax.experimental import pallas as pl
from jax.experimental.pallas import tpu as pltpu
from jax.sharding import PartitionSpec as P

EXPERTS = 8
CAP = 36
PIECE = 2 * CAP
KINDS = ("x", "dz")
MIB = 1 << 20
VMEM = pl.BlockSpec(memory_space=pltpu.VMEM)


def dot(left, right, dims=((1,), (0,))):
    return lax.dot_general(left, right, (dims, ((), ())), preferred_element_type=jnp.float32)


def params(mib):
    return pltpu.CompilerParams(vmem_limit_bytes=mib * MIB)


def cost(flops, moved):
    return pl.CostEstimate(flops=int(flops), bytes_accessed=int(moved), transcendentals=0)


def send_layout(groups, share, part, kinds):
    if groups != 4:
        return [(k, [(kind, k, 0, share) for kind in kinds] + [("part", 0, 0, part)]) for k in range(1, groups)], 0
    half, cut = part // 2, share // 2
    left, right = ("part", 0, 0, half), ("part", 0, half, half)
    over_x = [(kind, 1, 0, share) for kind in kinds] + [right, left] + [(kind, 3, 0, cut) for kind in kinds]
    over_y = [(kind, 2, 0, share) for kind in kinds] + [left, right] + [(kind, 3, cut, cut) for kind in kinds]
    return [(1, over_x), (2, over_y)], half + cut * len(kinds)


def own_fields(share, part, kinds):
    return [(kind, 0, 0, share) for kind in kinds] + [("part", 0, 0, part)]


def all_layouts(groups, share, part, kinds):
    return [own_fields(share, part, kinds)] + [f for _, f in send_layout(groups, share, part, kinds)[0]]


def fields_width(fields):
    return sum(field[3] for field in fields)


def received(groups, share, part, kinds):
    messages, relayed = send_layout(groups, share, part, kinds)
    result = []
    for index, (sent, fields) in enumerate([(0, own_fields(share, part, kinds))] + messages):
        column, found = 0, {}
        for kind, offset, first, count in fields:
            if kind == "part" or offset == sent:
                found.setdefault(kind, []).append((index, column, first, count))
            column += count
        found["part"].sort(key=lambda f: f[2])
        result.append(found)
    if relayed:
        half, cut = part // 2, share // 2
        found = {"part": [(3, 0, 0, half), (4, 0, half, half)]}
        for i, kind in enumerate(kinds):
            found[kind] = [(3, half + i * cut, 0, cut), (4, half + i * cut, cut, cut)]
        result.append(found)
    return result


def store_rows(outs, layouts, want, source, top, share):
    me = lax.axis_index("dp")
    for out, fields in zip(outs, layouts):
        column = 0
        for kind, offset, first, count in fields:
            if kind == want:
                start = pl.multiple_of((me ^ offset) * share + first, 128)
                out[:, column : column + count] = source[top : top + PIECE, pl.ds(start, count)]
            column += count


def store_part(outs, layouts, step, tile, value, base=0):
    for out, fields in zip(outs, layouts):
        column = 0
        for kind, _, first, count in fields:
            if kind == "part":
                at = base + step * tile - first

                @pl.when((at >= 0) & (at < count))
                def _(out=out, column=column, at=at):
                    out[:, pl.ds(pl.multiple_of(column + at, 128), tile)] = value

            column += count


def partner_expert(k, tiles):
    d = lax.axis_index("expert")
    return (2 * (lax.shift_right_logical(d, 1) ^ k) + (d & 1)) // tiles


def slot_rows(routing, chips, tiles):
    tok = routing.shape[1] // 2
    r0, r1, g0, g1 = (routing[i : i + 1, :] for i in range(4))
    before = (
        lax.broadcasted_iota(jnp.int32, (tok, tok), 0) < lax.broadcasted_iota(jnp.int32, (tok, tok), 1)
    ).astype(jnp.bfloat16)
    lane = lax.broadcasted_iota(jnp.int32, (1, 2 * tok), 1)
    base = jnp.where(lane >= tok, CAP, 0)
    result = []
    for k in range(chips):
        expert = partner_expert(k, tiles)
        first, second = r0 == expert, r1 == expert
        named = (first | second).astype(jnp.float32)
        flags = jnp.broadcast_to(named, (8, 2 * tok)).astype(jnp.bfloat16)
        position = jnp.concatenate(
            [dot(flags[:, :tok], before), dot(flags[:, tok:], before)], axis=1
        )[0:1]
        row = position.astype(jnp.int32) + base + k * PIECE
        gate = jnp.where(first, g0, g1)
        result.append((jnp.where(named > 0, row, -1), gate))
    return result


def dispatch_kernel(chips, tiles, routing_ref, other_routing_ref, x_ref, other_x_ref, dy_ref, other_dy_ref, *out_refs):
    tok, width = x_ref.shape
    routing = jnp.concatenate([routing_ref[...], other_routing_ref[...]], axis=1)
    slots = chips * PIECE
    row_id = lax.broadcasted_iota(jnp.int32, (slots, 2 * tok), 0)
    chosen = jnp.zeros((slots, 2 * tok), jnp.float32)
    factor = jnp.zeros((slots, 2 * tok), jnp.float32)
    for row, gate in slot_rows(routing, chips, tiles):
        hit = row_id == row
        chosen = jnp.where(hit, 1.0, chosen)
        factor = jnp.where(hit, gate.astype(jnp.float32), factor)
    pick = chosen.astype(jnp.bfloat16)
    scale = jnp.sum(factor, axis=1, keepdims=True) / 1024.0
    step = min(512, width)
    for col in range(0, width, step):
        columns = slice(col, col + step)
        x = dot(pick, jnp.concatenate([x_ref[:, columns], other_x_ref[:, columns]], axis=0))
        dz = scale * dot(pick, jnp.concatenate([dy_ref[:, columns], other_dy_ref[:, columns]], axis=0))
        for k in range(chips):
            rows = slice(k * PIECE, (k + 1) * PIECE)
            out_refs[k][:, columns] = jnp.concatenate([x[rows], dz[rows]], axis=0).astype(jnp.bfloat16)


def dispatch(routing, other_routing, x, other_x, dy, other_dy, chips, tiles):
    tok, width = x.shape
    slots = chips * PIECE
    return pl.pallas_call(
        functools.partial(dispatch_kernel, chips, tiles),
        out_shape=[jax.ShapeDtypeStruct((2 * PIECE, width), jnp.bfloat16)] * chips,
        in_specs=[VMEM] * 6,
        out_specs=[VMEM] * chips,
        compiler_params=params(24),
        cost_estimate=cost(8 * slots * tok * width, 4 * (2 * x.size + slots * width)),
        name="dispatch",
    )(routing, other_routing, *in_hbm(x), other_x, *in_hbm(dy), other_dy)


def combine_kernel(chips, tiles, scaled, routing_ref, other_routing_ref, *refs):
    backs, own_ref, other_ref = refs[:chips], refs[chips], refs[chips + 1]
    tok, width = own_ref.shape
    routing = jnp.concatenate([routing_ref[...], other_routing_ref[...]], axis=1)
    slots = chips * PIECE
    row_id = lax.broadcasted_iota(jnp.int32, (slots, 2 * tok), 0)
    high = jnp.zeros((slots, 2 * tok), jnp.float32)
    low = jnp.zeros((slots, 2 * tok), jnp.float32)
    for row, gate in slot_rows(routing, chips, tiles):
        hit = row_id == row
        if scaled:
            rest = gate & 3
            high = jnp.where(hit, (gate - rest).astype(jnp.float32), high)
            low = jnp.where(hit, rest.astype(jnp.float32), low)
        else:
            high = jnp.where(hit, 1.0, high)
    high = high.astype(jnp.bfloat16)
    low = low.astype(jnp.bfloat16)
    step, lo = min(512, width), 0 if scaled else PIECE
    for col in range(0, width, step):
        rows = jnp.concatenate([back[lo : lo + PIECE, col : col + step] for back in backs], axis=0)
        summed = dot(high, rows, ((0,), (0,)))
        if scaled:
            summed = (summed + dot(low, rows, ((0,), (0,)))) / 1024.0
        own_ref[:, col : col + step] = summed[:tok]
        other_ref[:, col : col + step] = summed[tok:].astype(jnp.bfloat16)


def combine(routing, other_routing, backs, tiles, scaled):
    chips = len(backs)
    tok, width = routing.shape[1], backs[0].shape[1]
    return pl.pallas_call(
        functools.partial(combine_kernel, chips, tiles, scaled),
        out_shape=[jax.ShapeDtypeStruct((tok, width), kind) for kind in (jnp.float32, jnp.bfloat16)],
        in_specs=[VMEM] * (2 + chips),
        out_specs=[VMEM] * 2,
        compiler_params=params(24),
        cost_estimate=cost(4 * chips * PIECE * tok * width, 2 * chips * PIECE * width + 8 * tok * width),
        name="combine_mixed" if scaled else "combine_grad",
    )(routing, other_routing, *backs)


def add_to(total, part, step):
    @pl.when(step == 0)
    def _():
        total[...] = part

    @pl.when(step > 0)
    def _():
        total[...] += part


def experts_kernel(layouts, share, hidden, rows_ref, wg, wu, wd, back_ref, *refs):
    sends, (z_total, dx_total) = refs[: len(layouts)], refs[len(layouts) :]
    step, last = pl.program_id(0), pl.num_programs(0) - 1
    tile = wg.shape[1]

    @pl.when(step == 0)
    def _():
        store_rows(sends, layouts, "x", rows_ref, 0, share)
        store_rows(sends, layouts, "dz", rows_ref, PIECE, share)

    x, dz = rows_ref[:PIECE, :], rows_ref[PIECE:, :]
    a, b = dot(x, wg[...]), dot(x, wu[...])
    dh = dot(dz, wd[...], ((1,), (1,)))
    sig = jax.nn.sigmoid(a)
    act = a * sig
    h = (act * b).astype(jnp.bfloat16)
    d_gate = (dh * b * (sig * (1.0 + a * (1.0 - sig)))).astype(jnp.bfloat16)
    d_up = (dh * act).astype(jnp.bfloat16)
    store_part(sends, layouts, step, tile, h, 0)
    store_part(sends, layouts, step, tile, d_gate, hidden)
    store_part(sends, layouts, step, tile, d_up, 2 * hidden)
    add_to(z_total, dot(h, wd[...]), step)
    add_to(dx_total, dot(d_gate, wg[...], ((1,), (1,))) + dot(d_up, wu[...], ((1,), (1,))), step)

    @pl.when(step == last)
    def _():
        back_ref[...] = jnp.concatenate([z_total[...], dx_total[...]], axis=0).astype(jnp.bfloat16)


def whole(shape):
    return pl.BlockSpec(shape, lambda i: (0, 0))


def in_hbm(*weights):
    return [pltpu.with_memory_space_constraint(w, pltpu.HBM) for w in weights]


def hidden_tile(hidden):
    return 512 if hidden % 512 == 0 else hidden


def experts(rows, weights, groups):
    width, hidden = weights[0].shape
    tile, share = hidden_tile(hidden), width // groups
    layouts = all_layouts(groups, share, 3 * hidden, KINDS)
    sends = [(PIECE, fields_width(fields)) for fields in layouts]
    columns = pl.BlockSpec((width, tile), lambda i: (0, i))
    results = pl.pallas_call(
        functools.partial(experts_kernel, layouts, share, hidden),
        grid=(hidden // tile,),
        out_shape=[jax.ShapeDtypeStruct((2 * PIECE, width), jnp.bfloat16)]
        + [jax.ShapeDtypeStruct(shape, jnp.bfloat16) for shape in sends],
        in_specs=[whole((2 * PIECE, width)), columns, columns, pl.BlockSpec((tile, width), lambda i: (i, 0))],
        out_specs=[whole((2 * PIECE, width))] + [whole(shape) for shape in sends],
        scratch_shapes=[pltpu.VMEM((PIECE, width), jnp.float32)] * 2,
        compiler_params=params(28),
        cost_estimate=cost(12 * PIECE * width * hidden, 6 * width * hidden),
        name="experts",
    )(rows, *in_hbm(*weights))
    return results[0], list(results[1:])


def take(refs, fields):
    return jnp.concatenate([refs[i][:, column : column + count] for i, column, _, count in fields], axis=1)


def take_tile(refs, fields, lo, tile):
    for i, column, first, count in fields:
        if first <= lo < first + count:
            return refs[i][:, column + lo - first : column + lo - first + tile]


def weight_kernel(plan, partial, final, *refs):
    count = len(refs) - (7 if final else 3)
    arrays, outs = refs[:count], refs[count : count + 3]
    results, sems = (refs[count + 3 : count + 6], refs[count + 6]) if final else (outs, None)
    share, hidden = results[0].shape
    tile = min(256, hidden)
    x = jnp.concatenate([take(arrays, found["x"]) for found in plan], axis=0)
    dz = jnp.concatenate([take(arrays, found["dz"]) for found in plan], axis=0)
    copies = []

    def part(lo):
        return jnp.concatenate([take_tile(arrays, found["part"], lo, tile) for found in plan], axis=0)

    def put(which, rows, columns, left, right):
        value = dot(left, right, ((0,), (0,)))
        if partial:
            value = value + arrays[which][rows, columns]
        results[which][rows, columns] = value
        if final:
            to = outs[which].at[rows, columns]
            copies.append(pltpu.make_async_copy(results[which].at[rows, columns], to, sems.at[len(copies)]))
            copies[-1].start()

    for col in range(0, hidden, tile):
        part_of, whole_of = pl.ds(col, tile), pl.ds(0, share)
        put(0, whole_of, part_of, x, part(hidden + col))
        put(1, whole_of, part_of, x, part(2 * hidden + col))
        put(2, part_of, whole_of, part(col), dz)
    for copy in copies:
        copy.wait()


def weight_grads(sources, partial, final, share, hidden):
    arrays, plan = list(partial), []
    for have, found in sources:
        used = sorted({field[0] for fields in found.values() for field in fields})
        at = {index: len(arrays) + i for i, index in enumerate(used)}
        arrays += [have[index] for index in used]
        plan.append({kind: [(at[f[0]], *f[1:]) for f in fields] for kind, fields in found.items()})
    rows = len(sources) * PIECE
    shapes = [(share, hidden), (share, hidden), (hidden, share)]
    scratch = [pltpu.VMEM(shape, jnp.float32) for shape in shapes]
    scratch += [pltpu.SemaphoreType.DMA((3 * hidden // min(256, hidden),))]
    return pl.pallas_call(
        functools.partial(weight_kernel, plan, bool(partial), final),
        out_shape=[jax.ShapeDtypeStruct(shape, jnp.float32) for shape in shapes],
        in_specs=[VMEM] * len(arrays),
        out_specs=[pl.BlockSpec(memory_space=pl.ANY) if final else VMEM] * 3,
        scratch_shapes=scratch if final else [],
        compiler_params=params(48),
        cost_estimate=cost(6 * rows * share * hidden, 12 * share * hidden + 2 * rows * (2 * share + 3 * hidden)),
        name="weight_grads" if final else "weight_grads_early",
    )(*arrays)


def per_device(tokens, routes, gates, cotangent, w_gate, w_up, w_down):
    devices, groups = lax.axis_size("expert"), lax.axis_size("dp")
    chips, tiles = devices // 2, devices // EXPERTS
    width, hidden = w_gate.shape
    share = width // groups

    def swap(v):
        return lax.ppermute(v, "expert", [(i, i ^ 1) for i in range(devices)])

    def over_z(v, k):
        return lax.ppermute(v, "expert", [(i, i ^ (2 * k)) for i in range(devices)]) if k else v

    def over_dp(v, k):
        return lax.ppermute(v, "dp", [(i, i ^ k) for i in range(groups)]) if k else v

    def after(values, *others):
        return lax.optimization_barrier((values, others))[0]

    messages, relayed = send_layout(groups, share, 3 * hidden, KINDS)

    def first_phase(sends):
        return [sends[0]] + [over_dp(v, k) for v, (k, _) in zip(sends[1:], messages)]

    def second_phase(first, second):
        if relayed:
            for index, k in ((1, 2), (2, 1)):
                both = jnp.concatenate([first[index][:, -relayed:], second[index][:, -relayed:]], axis=0)
                both = over_dp(both, k)
                first.append(both[:PIECE])
                second.append(both[PIECE:])
        return first, second

    routing = jnp.concatenate([routes.T, gates.T], axis=0)
    other_routing = swap(routing)
    out = dispatch(routing, other_routing, tokens, swap(tokens), cotangent, swap(cotangent), chips, tiles)
    weights = (w_gate, w_up, w_down)
    order = [0, 1] + list(range(chips - 1, 1, -1))
    rows = {k: over_z(out[k], k) for k in order}
    back, sets, previous = {}, [], []
    last, early = order[-1], order[-2]
    for k in order[:-1]:
        back[k], sends = experts(after(rows[k], *previous), weights, groups)
        if len(sets) == 2:
            sends = after(sends, *sets[0])
        sets.append(first_phase(sends))
        previous = [back[k]]
    back[1] = after(back[1], back[early])
    got = {0: back[0]}
    got[1] = over_z(back[1], 1)
    got.update({k: over_z(back[k], k) for k in order[1:-1] if k != 1})
    back[last], sends = experts(after(rows[last], *previous, *sets[0], *sets[1]), weights, groups)
    back[last] = after(back[last], got[1])
    got[last] = over_z(back[last], last)
    sets[:2] = second_phase(*sets[:2])
    sends = after(sends, *sets[2])
    sets.append(first_phase(sends))
    sets[2:4] = second_phase(*sets[2:4])
    fields = received(groups, share, 3 * hidden, KINDS)
    sources = [(one, found) for one in sets for found in fields]
    cut = (len(sets) - 2) * len(fields) + (len(fields) - 1) * 1
    early_grads = weight_grads(sources[:cut], [], False, share, hidden)
    grads = weight_grads(sources[cut:], early_grads, True, share, hidden)
    back = after([got[k] for k in range(chips)], *grads)

    def finish(scaled):
        mine, theirs = combine(routing, other_routing, back, tiles, scaled)
        return (mine + swap(theirs)).astype(jnp.bfloat16)

    mixed, input_grad = finish(True), finish(False)
    return (mixed, input_grad, *grads)


def solution(mesh):
    rows = P(("dp", "expert"), None)
    in_specs = (rows, rows, rows, rows, P(None, "expert"), P(None, "expert"), P("expert", None))
    out_specs = (rows, rows, P("dp", "expert"), P("dp", "expert"), P("expert", "dp"))
    return jax.shard_map(
        per_device, mesh=mesh, in_specs=in_specs, out_specs=out_specs, check_vma=False
    )
```

```python
import functools

import jax
import jax.numpy as jnp
from jax import lax
from jax.experimental import pallas as pl
from jax.experimental.pallas import tpu as pltpu
from jax.sharding import PartitionSpec as P

EXPERTS = 8
CAP = 36
PIECE = 2 * CAP
KINDS = ("x", "dz")
MIB = 1 << 20
VMEM = pl.BlockSpec(memory_space=pltpu.VMEM)


def dot(left, right, dims=((1,), (0,))):
    return lax.dot_general(left, right, (dims, ((), ())), preferred_element_type=jnp.float32)


def params(mib):
    return pltpu.CompilerParams(vmem_limit_bytes=mib * MIB)


def cost(flops, moved):
    return pl.CostEstimate(flops=int(flops), bytes_accessed=int(moved), transcendentals=0)


def send_layout(groups, share, part, kinds):
    if groups != 4:
        return [(k, [(kind, k, 0, share) for kind in kinds] + [("part", 0, 0, part)]) for k in range(1, groups)], 0
    half, cut = part // 2, share // 2
    left, right = ("part", 0, 0, half), ("part", 0, half, half)
    over_x = [(kind, 1, 0, share) for kind in kinds] + [right, left] + [(kind, 3, 0, cut) for kind in kinds]
    over_y = [(kind, 2, 0, share) for kind in kinds] + [left, right] + [(kind, 3, cut, cut) for kind in kinds]
    return [(1, over_x), (2, over_y)], half + cut * len(kinds)


def own_fields(share, part, kinds):
    return [(kind, 0, 0, share) for kind in kinds] + [("part", 0, 0, part)]


def all_layouts(groups, share, part, kinds):
    return [own_fields(share, part, kinds)] + [f for _, f in send_layout(groups, share, part, kinds)[0]]


def fields_width(fields):
    return sum(field[3] for field in fields)


def received(groups, share, part, kinds):
    messages, relayed = send_layout(groups, share, part, kinds)
    result = []
    for index, (sent, fields) in enumerate([(0, own_fields(share, part, kinds))] + messages):
        column, found = 0, {}
        for kind, offset, first, count in fields:
            if kind == "part" or offset == sent:
                found.setdefault(kind, []).append((index, column, first, count))
            column += count
        found["part"].sort(key=lambda f: f[2])
        result.append(found)
    if relayed:
        half, cut = part // 2, share // 2
        found = {"part": [(3, 0, 0, half), (4, 0, half, half)]}
        for i, kind in enumerate(kinds):
            found[kind] = [(3, half + i * cut, 0, cut), (4, half + i * cut, cut, cut)]
        result.append(found)
    return result


def store_rows(outs, layouts, want, source, top, share):
    me = lax.axis_index("dp")
    for out, fields in zip(outs, layouts):
        column = 0
        for kind, offset, first, count in fields:
            if kind == want:
                start = pl.multiple_of((me ^ offset) * share + first, 128)
                out[:, column : column + count] = source[top : top + PIECE, pl.ds(start, count)]
            column += count


def store_part(outs, layouts, step, tile, value, base=0):
    for out, fields in zip(outs, layouts):
        column = 0
        for kind, _, first, count in fields:
            if kind == "part":
                at = base + step * tile - first

                @pl.when((at >= 0) & (at < count))
                def _(out=out, column=column, at=at):
                    out[:, pl.ds(pl.multiple_of(column + at, 128), tile)] = value

            column += count


def partner_expert(k, tiles):
    d = lax.axis_index("expert")
    return (2 * (lax.shift_right_logical(d, 1) ^ k) + (d & 1)) // tiles


def slot_rows(routing, chips, tiles):
    tok = routing.shape[1] // 2
    r0, r1, g0, g1 = (routing[i : i + 1, :] for i in range(4))
    before = (
        lax.broadcasted_iota(jnp.int32, (tok, tok), 0) < lax.broadcasted_iota(jnp.int32, (tok, tok), 1)
    ).astype(jnp.bfloat16)
    lane = lax.broadcasted_iota(jnp.int32, (1, 2 * tok), 1)
    base = jnp.where(lane >= tok, CAP, 0)
    result = []
    for k in range(chips):
        expert = partner_expert(k, tiles)
        first, second = r0 == expert, r1 == expert
        named = (first | second).astype(jnp.float32)
        flags = jnp.broadcast_to(named, (8, 2 * tok)).astype(jnp.bfloat16)
        position = jnp.concatenate(
            [dot(flags[:, :tok], before), dot(flags[:, tok:], before)], axis=1
        )[0:1]
        row = position.astype(jnp.int32) + base + k * PIECE
        gate = jnp.where(first, g0, g1)
        result.append((jnp.where(named > 0, row, -1), gate))
    return result


def dispatch_kernel(chips, tiles, routing_ref, other_routing_ref, x_ref, other_x_ref, dy_ref, other_dy_ref, *out_refs):
    tok, width = x_ref.shape
    routing = jnp.concatenate([routing_ref[...], other_routing_ref[...]], axis=1)
    slots = chips * PIECE
    row_id = lax.broadcasted_iota(jnp.int32, (slots, 2 * tok), 0)
    chosen = jnp.zeros((slots, 2 * tok), jnp.float32)
    factor = jnp.zeros((slots, 2 * tok), jnp.float32)
    for row, gate in slot_rows(routing, chips, tiles):
        hit = row_id == row
        chosen = jnp.where(hit, 1.0, chosen)
        factor = jnp.where(hit, gate.astype(jnp.float32), factor)
    pick = chosen.astype(jnp.bfloat16)
    scale = jnp.sum(factor, axis=1, keepdims=True) / 1024.0
    step = min(512, width)
    for col in range(0, width, step):
        columns = slice(col, col + step)
        x = dot(pick, jnp.concatenate([x_ref[:, columns], other_x_ref[:, columns]], axis=0))
        dz = scale * dot(pick, jnp.concatenate([dy_ref[:, columns], other_dy_ref[:, columns]], axis=0))
        for k in range(chips):
            rows = slice(k * PIECE, (k + 1) * PIECE)
            out_refs[k][:, columns] = jnp.concatenate([x[rows], dz[rows]], axis=0).astype(jnp.bfloat16)


def dispatch(routing, other_routing, x, other_x, dy, other_dy, chips, tiles):
    tok, width = x.shape
    slots = chips * PIECE
    return pl.pallas_call(
        functools.partial(dispatch_kernel, chips, tiles),
        out_shape=[jax.ShapeDtypeStruct((2 * PIECE, width), jnp.bfloat16)] * chips,
        in_specs=[VMEM] * 6,
        out_specs=[VMEM] * chips,
        compiler_params=params(24),
        cost_estimate=cost(8 * slots * tok * width, 4 * (2 * x.size + slots * width)),
        name="dispatch",
    )(routing, other_routing, *in_hbm(x), other_x, *in_hbm(dy), other_dy)


def combine_kernel(chips, tiles, scaled, routing_ref, other_routing_ref, *refs):
    backs, own_ref, other_ref = refs[:chips], refs[chips], refs[chips + 1]
    tok, width = own_ref.shape
    routing = jnp.concatenate([routing_ref[...], other_routing_ref[...]], axis=1)
    slots = chips * PIECE
    row_id = lax.broadcasted_iota(jnp.int32, (slots, 2 * tok), 0)
    high = jnp.zeros((slots, 2 * tok), jnp.float32)
    low = jnp.zeros((slots, 2 * tok), jnp.float32)
    for row, gate in slot_rows(routing, chips, tiles):
        hit = row_id == row
        if scaled:
            rest = gate & 3
            high = jnp.where(hit, (gate - rest).astype(jnp.float32), high)
            low = jnp.where(hit, rest.astype(jnp.float32), low)
        else:
            high = jnp.where(hit, 1.0, high)
    high = high.astype(jnp.bfloat16)
    low = low.astype(jnp.bfloat16)
    step, lo = min(512, width), 0 if scaled else PIECE
    for col in range(0, width, step):
        rows = jnp.concatenate([back[lo : lo + PIECE, col : col + step] for back in backs], axis=0)
        summed = dot(high, rows, ((0,), (0,)))
        if scaled:
            summed = (summed + dot(low, rows, ((0,), (0,)))) / 1024.0
        own_ref[:, col : col + step] = summed[:tok]
        other_ref[:, col : col + step] = summed[tok:].astype(jnp.bfloat16)


def combine(routing, other_routing, backs, tiles, scaled):
    chips = len(backs)
    tok, width = routing.shape[1], backs[0].shape[1]
    return pl.pallas_call(
        functools.partial(combine_kernel, chips, tiles, scaled),
        out_shape=[jax.ShapeDtypeStruct((tok, width), kind) for kind in (jnp.float32, jnp.bfloat16)],
        in_specs=[VMEM] * (2 + chips),
        out_specs=[VMEM] * 2,
        compiler_params=params(24),
        cost_estimate=cost(4 * chips * PIECE * tok * width, 2 * chips * PIECE * width + 8 * tok * width),
        name="combine_mixed" if scaled else "combine_grad",
    )(routing, other_routing, *backs)


def add_to(total, part, step):
    @pl.when(step == 0)
    def _():
        total[...] = part

    @pl.when(step > 0)
    def _():
        total[...] += part


def experts_kernel(layouts, share, hidden, rows_ref, wg, wu, wd, back_ref, *refs):
    sends, (z_total, dx_total) = refs[: len(layouts)], refs[len(layouts) :]
    step, last = pl.program_id(0), pl.num_programs(0) - 1
    tile = wg.shape[1]

    @pl.when(step == 0)
    def _():
        store_rows(sends, layouts, "x", rows_ref, 0, share)
        store_rows(sends, layouts, "dz", rows_ref, PIECE, share)

    x, dz = rows_ref[:PIECE, :], rows_ref[PIECE:, :]
    a, b = dot(x, wg[...]), dot(x, wu[...])
    dh = dot(dz, wd[...], ((1,), (1,)))
    sig = jax.nn.sigmoid(a)
    act = a * sig
    h = (act * b).astype(jnp.bfloat16)
    d_gate = (dh * b * (sig * (1.0 + a * (1.0 - sig)))).astype(jnp.bfloat16)
    d_up = (dh * act).astype(jnp.bfloat16)
    store_part(sends, layouts, step, tile, h, 0)
    store_part(sends, layouts, step, tile, d_gate, hidden)
    store_part(sends, layouts, step, tile, d_up, 2 * hidden)
    add_to(z_total, dot(h, wd[...]), step)
    add_to(dx_total, dot(d_gate, wg[...], ((1,), (1,))) + dot(d_up, wu[...], ((1,), (1,))), step)

    @pl.when(step == last)
    def _():
        back_ref[...] = jnp.concatenate([z_total[...], dx_total[...]], axis=0).astype(jnp.bfloat16)


def whole(shape):
    return pl.BlockSpec(shape, lambda i: (0, 0))


def in_hbm(*weights):
    return [pltpu.with_memory_space_constraint(w, pltpu.HBM) for w in weights]


def hidden_tile(hidden):
    return 512 if hidden % 512 == 0 else hidden


def experts(rows, weights, groups):
    width, hidden = weights[0].shape
    tile, share = hidden_tile(hidden), width // groups
    layouts = all_layouts(groups, share, 3 * hidden, KINDS)
    sends = [(PIECE, fields_width(fields)) for fields in layouts]
    columns = pl.BlockSpec((width, tile), lambda i: (0, i))
    results = pl.pallas_call(
        functools.partial(experts_kernel, layouts, share, hidden),
        grid=(hidden // tile,),
        out_shape=[jax.ShapeDtypeStruct((2 * PIECE, width), jnp.bfloat16)]
        + [jax.ShapeDtypeStruct(shape, jnp.bfloat16) for shape in sends],
        in_specs=[whole((2 * PIECE, width)), columns, columns, pl.BlockSpec((tile, width), lambda i: (i, 0))],
        out_specs=[whole((2 * PIECE, width))] + [whole(shape) for shape in sends],
        scratch_shapes=[pltpu.VMEM((PIECE, width), jnp.float32)] * 2,
        compiler_params=params(28),
        cost_estimate=cost(12 * PIECE * width * hidden, 6 * width * hidden),
        name="experts",
    )(rows, *in_hbm(*weights))
    return results[0], list(results[1:])


def take(refs, fields):
    return jnp.concatenate([refs[i][:, column : column + count] for i, column, _, count in fields], axis=1)


def take_tile(refs, fields, lo, tile):
    for i, column, first, count in fields:
        if first <= lo < first + count:
            return refs[i][:, column + lo - first : column + lo - first + tile]


def weight_kernel(plan, partial, final, *refs):
    count = len(refs) - (7 if final else 3)
    arrays, outs = refs[:count], refs[count : count + 3]
    results, sems = (refs[count + 3 : count + 6], refs[count + 6]) if final else (outs, None)
    share, hidden = results[0].shape
    tile = min(256, hidden)
    x = jnp.concatenate([take(arrays, found["x"]) for found in plan], axis=0)
    dz = jnp.concatenate([take(arrays, found["dz"]) for found in plan], axis=0)
    copies = []

    def part(lo):
        return jnp.concatenate([take_tile(arrays, found["part"], lo, tile) for found in plan], axis=0)

    def put(which, rows, columns, left, right):
        value = dot(left, right, ((0,), (0,)))
        if partial:
            value = value + arrays[which][rows, columns]
        results[which][rows, columns] = value
        if final:
            to = outs[which].at[rows, columns]
            copies.append(pltpu.make_async_copy(results[which].at[rows, columns], to, sems.at[len(copies)]))
            copies[-1].start()

    for col in range(0, hidden, tile):
        part_of, whole_of = pl.ds(col, tile), pl.ds(0, share)
        put(0, whole_of, part_of, x, part(hidden + col))
        put(1, whole_of, part_of, x, part(2 * hidden + col))
        put(2, part_of, whole_of, part(col), dz)
    for copy in copies:
        copy.wait()


def weight_grads(sources, partial, final, share, hidden):
    arrays, plan = list(partial), []
    for have, found in sources:
        used = sorted({field[0] for fields in found.values() for field in fields})
        at = {index: len(arrays) + i for i, index in enumerate(used)}
        arrays += [have[index] for index in used]
        plan.append({kind: [(at[f[0]], *f[1:]) for f in fields] for kind, fields in found.items()})
    rows = len(sources) * PIECE
    shapes = [(share, hidden), (share, hidden), (hidden, share)]
    scratch = [pltpu.VMEM(shape, jnp.float32) for shape in shapes]
    scratch += [pltpu.SemaphoreType.DMA((3 * hidden // min(256, hidden),))]
    return pl.pallas_call(
        functools.partial(weight_kernel, plan, bool(partial), final),
        out_shape=[jax.ShapeDtypeStruct(shape, jnp.float32) for shape in shapes],
        in_specs=[VMEM] * len(arrays),
        out_specs=[pl.BlockSpec(memory_space=pl.ANY) if final else VMEM] * 3,
        scratch_shapes=scratch if final else [],
        compiler_params=params(48),
        cost_estimate=cost(6 * rows * share * hidden, 12 * share * hidden + 2 * rows * (2 * share + 3 * hidden)),
        name="weight_grads" if final else "weight_grads_early",
    )(*arrays)


def per_device(tokens, routes, gates, cotangent, w_gate, w_up, w_down):
    devices, groups = lax.axis_size("expert"), lax.axis_size("dp")
    chips, tiles = devices // 2, devices // EXPERTS
    width, hidden = w_gate.shape
    share = width // groups

    def swap(v):
        return lax.ppermute(v, "expert", [(i, i ^ 1) for i in range(devices)])

    def over_z(v, k):
        return lax.ppermute(v, "expert", [(i, i ^ (2 * k)) for i in range(devices)]) if k else v

    def over_dp(v, k):
        return lax.ppermute(v, "dp", [(i, i ^ k) for i in range(groups)]) if k else v

    def after(values, *others):
        return lax.optimization_barrier((values, others))[0]

    messages, relayed = send_layout(groups, share, 3 * hidden, KINDS)

    def first_phase(sends):
        return [sends[0]] + [over_dp(v, k) for v, (k, _) in zip(sends[1:], messages)]

    def second_phase(first, second):
        if relayed:
            for index, k in ((1, 2), (2, 1)):
                both = jnp.concatenate([first[index][:, -relayed:], second[index][:, -relayed:]], axis=0)
                both = over_dp(both, k)
                first.append(both[:PIECE])
                second.append(both[PIECE:])
        return first, second

    routing = jnp.concatenate([routes.T, gates.T], axis=0)
    other_routing = swap(routing)
    out = dispatch(routing, other_routing, tokens, swap(tokens), cotangent, swap(cotangent), chips, tiles)
    weights = (w_gate, w_up, w_down)
    order = [0, 1] + list(range(chips - 1, 1, -1))
    rows = {k: over_z(out[k], k) for k in order}
    back, sets, previous = {}, [], []
    last, early = order[-1], order[-2]
    for k in order[:-1]:
        back[k], sends = experts(after(rows[k], *previous), weights, groups)
        if len(sets) == 2:
            sends = after(sends, *sets[0])
        sets.append(first_phase(sends))
        previous = [back[k]]
    back[1] = after(back[1], back[early])
    got = {0: back[0]}
    got[1] = over_z(back[1], 1)
    got.update({k: over_z(back[k], k) for k in order[1:-1] if k != 1})
    back[last], sends = experts(after(rows[last], *previous), weights, groups)
    back[last] = after(back[last], got[1])
    got[last] = over_z(back[last], last)
    sets[:2] = second_phase(*sets[:2])
    sends = after(sends, *sets[2])
    sets.append(first_phase(sends))
    sets[2:4] = second_phase(*sets[2:4])
    fields = received(groups, share, 3 * hidden, KINDS)
    sources = [(one, found) for one in sets for found in fields]
    cut = (len(sets) - 2) * len(fields) + (len(fields) - 1) * 1
    early_grads = weight_grads(sources[:cut], [], False, share, hidden)
    grads = weight_grads(sources[cut:], early_grads, True, share, hidden)
    back = after([got[k] for k in range(chips)], *grads)

    def finish(scaled):
        mine, theirs = combine(routing, other_routing, back, tiles, scaled)
        return (mine + swap(theirs)).astype(jnp.bfloat16)

    mixed, input_grad = finish(True), finish(False)
    return (mixed, input_grad, *grads)


def solution(mesh):
    rows = P(("dp", "expert"), None)
    in_specs = (rows, rows, rows, rows, P(None, "expert"), P(None, "expert"), P("expert", None))
    out_specs = (rows, rows, P("dp", "expert"), P("dp", "expert"), P("expert", "dp"))
    return jax.shard_map(
        per_device, mesh=mesh, in_specs=in_specs, out_specs=out_specs, check_vma=False
    )
```
